128 devices in a mesh: wide: 16 (over y, z_hi, core), local: 8 (over x, z_lo).
Axes of the slice: x: 4, y: 4, z: 4 (z_hi: 2, z_lo: 2; z = z_hi * 2 + z_lo), core: 2. Of those that a mesh axis runs over, the one named last changes fastest.
Arguments:
- grad_out: bfloat16 [16384, 2080], P(('wide', 'local')), may hold values from -6 to 6
- expert_id: int32 [16384], P(('wide', 'local')), may hold values from 0 to 15, as said below
- slot: int32 [16384], P(('wide', 'local')), may hold values from -1 to 7, as said below
- gate_prob: float32 [16384], P(('wide', 'local')), may hold values from 0.1 to 1
- saved_inputs: bfloat16 [16, 16, 64, 2080], P('wide', None, 'local'), may hold values from -6 to 6
- w_in: bfloat16 [16, 2080, 6144], P('wide', None, 'local'), may hold values from -0.125 to 0.125
- w_out: bfloat16 [16, 6144, 2080], P('wide', 'local'), may hold values from -0.078125 to 0.078125
Outputs:
- grad_tokens: bfloat16 [16384, 2080], P(('wide', 'local'))
- grad_in_weight: bfloat16 [16, 2080, 6144], P('wide', None, 'local')
- grad_out_weight: bfloat16 [16, 6144, 2080], P('wide', 'local')
The draws below stay inside these ranges and needn't reach their ends.
Inputs may be any that keep to these rules, and one draw needn't show every extreme that they name: `expert_id`: the expert each token chose. `slot`: the position of a token among the tokens of its device that chose the same expert, in token order, or -1 where that position is 8 or more. In every draw one expert, common to all devices, fills all 8 of its slots from every device.
All inputs are finite; a program needn't handle non-finite values.
Results may differ from the reference program's by a relative error of at most 0.014.
Values may be sent and summed in bfloat16 or wider, within the bound.
No kernel may reach another device: no remote copies, remote signals or barrier semaphores. Data moves between devices by JAX's collectives and lax.ppermute only.
A program may use at most 128 MiB of HBM per device.

```python
import math
import jax
import jax.numpy as jnp
from jax import lax

D = 2080
FF = 6144
TOK_DEV = 128
EXPERTS = 16
CAP = 8
TOKENS = 16384
N_WIDE = 16
N_LOCAL = 8


def routing(key):
    devices = TOKENS // TOK_DEV
    first, second, third = jax.random.split(key, 3)
    chosen = jax.random.randint(first, (devices, TOK_DEV), 0, EXPERTS)
    favourite = jax.random.randint(second, (), 0, EXPERTS)
    order = jax.vmap(lambda sub: jax.random.permutation(sub, TOK_DEV))(jax.random.split(third, devices))
    chosen = jnp.where(order < CAP, favourite, chosen).astype(jnp.int32)
    onehot = (chosen[:, :, None] == jnp.arange(EXPERTS, dtype=jnp.int32)[None, None, :]).astype(jnp.int32)
    before = jnp.cumsum(onehot, axis=1) - onehot
    ranking = jnp.sum(before * onehot, axis=2)
    places = jnp.where(ranking < CAP, ranking, -1).astype(jnp.int32)
    return (chosen.reshape(-1), places.reshape(-1))


def draw_expert_id(key, part):
    chosen, places = routing(key)
    return chosen


def draw_slot(key, part):
    chosen, places = routing(key)
    return places


def block_levels(rng, shape, shards, smallest, largest):
    def one(position, shards_of):
        heights = jax.random.uniform(jax.random.fold_in(jax.random.fold_in(rng, 6), position), (shards_of,), jnp.float32, smallest / len(shards), largest / len(shards))
        return jnp.repeat(jnp.exp(heights), shape[position] // shards_of).reshape((-1,) + (1,) * (len(shape) - position - 1))

    level = one(*shards[0])
    for cut in shards[1:]:
        level = level * one(*cut)
    return level


def bell_draw(rng, shape, spread, limit, cuts=(), kind=jnp.bfloat16):
    values = spread * jax.random.normal(rng, shape, jnp.float32)
    if cuts:
        values = values * block_levels(rng, shape, cuts, -0.22, 0.18)
    return jnp.clip(values, -limit, limit).astype(kind)


def setup_inputs(seed: int = 0) -> dict:
    keys = jax.random.split(jax.random.key(seed), 8)
    return {
        "grad_out": bell_draw(keys[0], (TOKENS, D), 1.0, 6.0, ((0, 128),)),
        "expert_id": draw_expert_id(jax.random.fold_in(keys[7], 71), 0),
        "slot": draw_slot(jax.random.fold_in(keys[7], 71), 0),
        "gate_prob": jnp.clip(jnp.exp(math.log(1.0) - 2.3025851 * jax.random.uniform(keys[3], (TOKENS,), jnp.float32) ** block_levels(keys[3], (TOKENS,), ((0, 128),), -0.2, 0.2)), 0.1, 1.0),
        "saved_inputs": bell_draw(keys[4], (EXPERTS, N_WIDE, N_LOCAL * CAP, D), 1.0, 6.0, ((0, 16), (2, 8))),
        "w_in": bell_draw(keys[5], (EXPERTS, D, FF), D ** -0.5, 0.125, ((0, 16), (2, 8))),
        "w_out": bell_draw(keys[6], (EXPERTS, FF, D), FF ** -0.5, 0.078125, ((0, 16), (1, 8))),
    }


def gelu_parts(value):
    normal_cdf = 0.5 * (1.0 + lax.erf(value * 0.7071067811865476))
    density = jnp.exp(-0.5 * value * value) * 0.3989422804014327
    return value * normal_cdf, normal_cdf + value * density


def expert_backward(pieces):
    rows, grads, first, second = pieces
    pre = jnp.dot(rows, first, preferred_element_type=jnp.float32)
    value, slope = gelu_parts(pre)
    hidden = value.astype(jnp.bfloat16)
    back = jnp.dot(grads, second.T, preferred_element_type=jnp.float32)
    dhidden = (back * slope).astype(jnp.bfloat16)
    grad_first = jnp.dot(rows.T, dhidden, preferred_element_type=jnp.float32).astype(jnp.bfloat16)
    grad_second = jnp.dot(hidden.T, grads, preferred_element_type=jnp.float32).astype(jnp.bfloat16)
    count = rows.shape[0]
    blocks = jnp.einsum("rkf,dkf->krd", dhidden.astype(jnp.float32).reshape(count, N_LOCAL, -1),
                        first.astype(jnp.float32).reshape(D, N_LOCAL, -1))
    rounded = lax.optimization_barrier(blocks.astype(jnp.bfloat16))
    summed = jnp.sum(rounded.astype(jnp.float32), axis=0).astype(jnp.bfloat16)
    return grad_first, grad_second, summed


def reference(grad_out, expert_id, slot, gate_prob, saved_inputs, w_in, w_out):
    devices = TOKENS // TOK_DEV
    kept = slot >= 0
    target = jnp.where(kept, expert_id * CAP + slot, 0).astype(jnp.int32)
    owner = (jnp.arange(TOKENS, dtype=jnp.int32) // TOK_DEV).astype(jnp.int32)
    scaled = (gate_prob[:, None] * grad_out.astype(jnp.float32)).astype(jnp.bfloat16)
    placed = jnp.where(kept[:, None], scaled.astype(jnp.float32), jnp.float32(0.0))
    buffer = jnp.zeros((devices, EXPERTS * CAP, D), jnp.float32).at[owner, target].add(placed)
    buffer = buffer.astype(jnp.bfloat16).reshape(N_WIDE, N_LOCAL, EXPERTS, CAP, D)
    incoming = jnp.transpose(buffer, (2, 0, 1, 3, 4)).reshape(EXPERTS, N_WIDE * N_LOCAL * CAP, D)
    inputs = saved_inputs.reshape(EXPERTS, N_WIDE * N_LOCAL * CAP, D)
    grad_in_weight, grad_out_weight, returned = lax.map(expert_backward, (inputs, incoming, w_in, w_out))
    returned = returned.reshape(EXPERTS, N_WIDE, N_LOCAL, CAP, D)
    returned = jnp.transpose(returned, (1, 2, 0, 3, 4)).reshape(devices, EXPERTS * CAP, D)
    picked = returned[owner, target]
    grad_tokens = jnp.where(kept[:, None], picked, jnp.zeros_like(picked))
    return grad_tokens, grad_in_weight, grad_out_weight
```

```python
import jax
import jax.numpy as jnp
from jax import lax
from jax.sharding import Mesh, PartitionSpec as P

AXES = ("y", "zh", "core", "x", "zl")
EXCHANGE = ("zl", "y", "zh")
RIGHT = [(i, (i + 1) % 4) for i in range(4)]
LEFT = [(i, (i - 1) % 4) for i in range(4)]
SWAP = [(0, 1), (1, 0)]


def gelu_parts(value):
    normal_cdf = 0.5 * (1.0 + lax.erf(value * 0.7071067811865476))
    density = jnp.exp(-0.5 * value * value) * 0.3989422804014327
    return (value * normal_cdf, normal_cdf + value * density)


def contract(left, right, left_dim, right_dim):
    return lax.dot_general(
        left, right, (((left_dim,), (right_dim,)), ((), ())), preferred_element_type=jnp.float32
    )


def right(value):
    return lax.ppermute(value, "x", RIGHT)


def left(value):
    return lax.ppermute(value, "x", LEFT)


def other_z(value):
    return lax.ppermute(value, "zl", SWAP)


def other_core(value):
    return lax.ppermute(value, "core", SWAP)


def gather_x(own):
    from_left = right(own)
    from_right = left(own)
    far_first = right(from_left[0])
    far_second = left(from_right[1])
    return [own, from_left, from_right, jnp.stack([far_first, far_second])]


def reduce_x(own, to_left, to_right, to_far):
    wide = jnp.float32
    far_first = right(to_far[0])
    far_second = left(to_far[1])
    to_right = jnp.stack([(to_right[0].astype(wide) + far_first).astype(jnp.bfloat16), to_right[1]])
    to_left = jnp.stack([to_left[0], (to_left[1].astype(wide) + far_second).astype(jnp.bfloat16)])
    from_left = right(to_right)
    from_right = left(to_left)
    return (own.astype(wide) + from_left + from_right).astype(jnp.bfloat16)


def per_device(grad_out, expert_id, slot, gate_prob, saved_inputs, w_in, w_out):
    core = lax.axis_index("core")
    z_here = lax.axis_index("zl")
    capacity, width = saved_inputs.shape[2:]
    first = w_in[0]
    second = w_out[0]

    kept = slot >= 0
    target = ((expert_id % 2 + core) % 2) * 8 * capacity + (expert_id // 2) * capacity + slot
    columns = jnp.arange(16 * capacity, dtype=jnp.int32)
    placing = ((target[:, None] == columns[None, :]) & kept[:, None]).astype(jnp.bfloat16)
    scaled = (gate_prob[:, None] * grad_out.astype(jnp.float32)).astype(jnp.bfloat16)
    outgoing = contract(placing, scaled, 0, 0).astype(jnp.bfloat16).reshape(2, 8, capacity, width)

    def relative(value):
        return jnp.where(z_here == 0, value, value[::-1])

    def dispatch(part):
        copies = jnp.broadcast_to(outgoing[part][None], (2, 8, capacity, width))
        copies = copies.reshape(16, capacity, width)
        if part == 1:
            copies = other_core(copies)
        arrived = lax.all_to_all(copies, EXCHANGE, split_axis=0, concat_axis=0, tiled=True)
        return relative(arrived.reshape(2, 8 * capacity, width))

    inputs = saved_inputs[0].reshape(8, 2, capacity, width)
    inputs = jnp.where(core == 0, inputs, inputs[:, ::-1]).transpose(1, 0, 2, 3).reshape(2, 8 * capacity, width)
    near = gather_x(inputs)
    far = [other_z(piece) for piece in near]
    cotangents = [jnp.stack(gather_x(dispatch(part))).reshape(-1, width) for part in range(2)]
    every = jnp.stack([jnp.stack(near), jnp.stack(far)], axis=1)
    rows = [every[:, :, part].reshape(-1, width) for part in range(2)]

    sums = []
    hiddens = []
    dhiddens = []
    for part in range(2):
        pre = jnp.dot(rows[part], first, preferred_element_type=jnp.float32)
        value, slope = gelu_parts(pre)
        hiddens.append(value.astype(jnp.bfloat16))
        back = contract(cotangents[part], second, 1, 1)
        dhidden = (back * slope).astype(jnp.bfloat16)
        dhiddens.append(dhidden)
        partial_value = contract(dhidden, first, 1, 1).astype(jnp.bfloat16)
        own, to_left, to_right, to_far = partial_value.reshape(4, 2, 8 * capacity, width)
        total = relative(reduce_x(own, to_left, to_right, to_far))
        back_home = lax.all_to_all(
            total.reshape(16, capacity, width), EXCHANGE, split_axis=0, concat_axis=0, tiled=True
        ).reshape(2, 8 * capacity, width)
        summed = (back_home[0].astype(jnp.float32) + back_home[1]).astype(jnp.bfloat16)
        if part == 1:
            summed = other_core(summed)
        sums.append(summed)

    grad_out_weight = contract(
        jnp.concatenate(hiddens), jnp.concatenate(cotangents), 0, 0
    ).astype(jnp.bfloat16)[None]
    grad_in_weight = contract(
        jnp.concatenate(rows), jnp.concatenate(dhiddens), 0, 0
    ).astype(jnp.bfloat16)[None]
    grad_tokens = jnp.dot(placing, jnp.concatenate(sums), preferred_element_type=jnp.float32).astype(
        jnp.bfloat16
    )
    return (grad_tokens, grad_in_weight, grad_out_weight)


def solution(mesh):
    fine = Mesh(mesh.devices.reshape(4, 2, 2, 4, 2), AXES)
    wide = ("y", "zh", "core")
    local = ("x", "zl")
    placed = (
        P(wide + local, None),
        P(wide + local),
        P(wide + local),
        P(wide + local),
        P(wide, None, local, None),
        P(wide, None, local),
        P(wide, local, None),
    )
    return jax.shard_map(
        per_device,
        mesh=fine,
        in_specs=placed,
        out_specs=(P(wide + local, None), P(wide, None, local), P(wide, local, None)),
        check_vma=False,
    )
```

```python
import jax
import jax.numpy as jnp
from jax import lax
from jax.experimental import pallas as pl
from jax.experimental.pallas import tpu as pltpu
from jax.sharding import Mesh, PartitionSpec as P

AXES = ("y", "zh", "core", "x", "zl")
EXCHANGE = ("core", "zl", "y", "zh")
RIGHT = [(i, (i + 1) % 4) for i in range(4)]
LEFT = [(i, (i - 1) % 4) for i in range(4)]
SWAP = [(0, 1), (1, 0)]
BF = jnp.bfloat16
F32 = jnp.float32
VMEM = pl.BlockSpec(memory_space=pltpu.VMEM)
ANY = pl.BlockSpec(memory_space=pl.ANY)
PARAMS = pltpu.CompilerParams(vmem_limit_bytes=50 * 1024 * 1024)


def dot(a, b, da, db):
    return lax.dot_general(a, b, (((da,), (db,)), ((), ())), preferred_element_type=F32)


def cost(flops, nbytes):
    return pl.CostEstimate(flops=flops, bytes_accessed=nbytes, transcendentals=0)


def placing_of(expert, slot):
    target = (expert % 2) * 64 + (expert // 2) * 8 + slot
    target = jnp.where(slot >= 0, target, -1)
    columns = lax.broadcasted_iota(jnp.int32, (128, 128), 0)
    return jnp.where(columns == target, 1.0, 0.0).astype(BF)


def prepare_kernel(grad_ref, expert_ref, slot_ref, gate_ref, saved_ref, out_ref, own_ref):
    scaled = (gate_ref[...] * grad_ref[...].astype(F32)).astype(BF)
    placing = placing_of(expert_ref[...], slot_ref[...])
    outgoing = dot(placing, scaled, 1, 1).astype(BF)
    for core in range(2):
        for copy in range(2):
            out_ref[pl.ds(core * 128 + copy * 64, 64), :] = outgoing[core * 64 : core * 64 + 64]
    to = lax.broadcasted_iota(jnp.int32, (128, 128), 0)
    source = ((to % 64) // 8) * 16 + (to // 64) * 8 + to % 8
    columns = lax.broadcasted_iota(jnp.int32, (128, 128), 1)
    order = jnp.where(columns == source, 1.0, 0.0).astype(BF)
    own_ref[...] = dot(order, saved_ref[...], 1, 0).astype(BF)


def prepare(grad_t, expert, slot, gate, saved):
    width = saved.shape[1]
    return pl.pallas_call(
        prepare_kernel,
        out_shape=(jax.ShapeDtypeStruct((256, width), BF), jax.ShapeDtypeStruct((128, width), BF)),
        in_specs=[VMEM] * 5,
        out_specs=(VMEM, VMEM),
        compiler_params=PARAMS,
        cost_estimate=cost(2 * 2 * 128 * 128 * width, 5 * 128 * width * 2),
        name="prepare",
    )(grad_t, expert, slot, gate, saved)


def gelu_parts(value):
    normal_cdf = 0.5 * (1.0 + lax.erf(value * 0.7071067811865476))
    density = jnp.exp(-0.5 * value * value) * 0.3989422804014327
    return value * normal_cdf, normal_cdf + value * density


def forward_kernel(z_ref, own, lft, rgt, far0, far1, zown, zlft, zrgt, zfar0, zfar1, w_ref,
                   rows_ref, hidden_ref, slope_ref, sems):
    z = z_ref[0]
    copies = []

    def load(src, part, rel, here):
        zl = z if here else 1 - z
        start = pl.multiple_of(part * 512 + rel * 128 + zl * 64, 64)
        copies.append(pltpu.make_async_copy(src, rows_ref.at[pl.ds(start, 64), :], sems.at[len(copies)]))

    for part in range(2):
        for rel, (mine, other) in enumerate(((own, zown), (lft, zlft), (rgt, zrgt))):
            load(mine.at[pl.ds(part * 64, 64), :], part, rel, True)
            load(other.at[pl.ds(part * 64, 64), :], part, rel, False)
        load((far0, far1)[part], part, 3, True)
        load((zfar0, zfar1)[part], part, 3, False)
    for copy in copies:
        copy.start()
    for part in range(2):
        for copy in copies[part * 8 : part * 8 + 8]:
            copy.wait()
        for block in range(2):
            at = pl.ds(part * 512 + block * 256, 256)
            pre = dot(rows_ref[at, :], w_ref[...], 1, 0)
            value, slope = gelu_parts(pre)
            hidden_ref[at, :] = value.astype(BF)
            slope_ref[at, :] = slope


def forward(z, pieces, w_in):
    width, units = w_in.shape
    return pl.pallas_call(
        forward_kernel,
        out_shape=(
            jax.ShapeDtypeStruct((1024, width), BF),
            jax.ShapeDtypeStruct((1024, units), BF),
            jax.ShapeDtypeStruct((1024, units), F32),
        ),
        in_specs=[pl.BlockSpec(memory_space=pltpu.SMEM)] + [ANY] * 10 + [VMEM],
        out_specs=(VMEM, VMEM, VMEM),
        scratch_shapes=[pltpu.SemaphoreType.DMA((16,))],
        compiler_params=PARAMS,
        cost_estimate=cost(2 * 1024 * width * units, 20 << 20),
        name="forward",
    )(z, *pieces, w_in)


def backward_kernel(own, lft, rgt, far0, far1, slope_ref, wo_ref, wi_ref,
                    rows_ref, dhidden_ref, pown, plft, prgt, pfar0, pfar1, sems):
    copies = []
    sources = ((own, 0, 128), (lft, 128, 128), (rgt, 256, 128), (far0, 384, 64), (far1, 448, 64))
    for src, start, size in sources:
        copies.append(pltpu.make_async_copy(src, rows_ref.at[pl.ds(start, size), :], sems.at[len(copies)]))
    for copy in copies:
        copy.start()
    for copy in copies:
        copy.wait()
    for block in (1, 0):
        at = pl.ds(block * 256, 256)
        back = dot(rows_ref[at, :], wo_ref[...], 1, 0)
        dhidden = (back * slope_ref[at, :]).astype(BF)
        dhidden_ref[at, :] = dhidden
        partial_value = dot(dhidden, wi_ref[...], 1, 1).astype(BF)
        if block == 1:
            prgt[...] = partial_value[:128]
            pfar0[...] = partial_value[128:192]
            pfar1[...] = partial_value[192:]
        else:
            pown[...] = partial_value[:128]
            plft[...] = partial_value[128:]


def backward(part, pieces, slope, w_out_t, w_in):
    width, units = w_in.shape
    whole = lambda shape: pl.BlockSpec(shape, lambda i: (0, 0))
    return pl.pallas_call(
        backward_kernel,
        grid=(1,),
        out_shape=tuple(
            jax.ShapeDtypeStruct(s, BF)
            for s in ((512, width), (512, units)) + ((128, width),) * 3 + ((64, width),) * 2
        ),
        in_specs=[ANY] * 5
        + [
            pl.BlockSpec((512, units), lambda i: (part, 0)),
            whole((width, units)),
            whole((width, units)),
        ],
        out_specs=tuple(
            whole(s) for s in ((512, width), (512, units)) + ((128, width),) * 3 + ((64, width),) * 2
        ),
        scratch_shapes=[pltpu.SemaphoreType.DMA((5,))],
        compiler_params=PARAMS,
        cost_estimate=cost(2 * 2 * 512 * width * units, 14 << 20),
        name="backward",
    )(*pieces, slope, w_out_t, w_in)


def middle_kernel(right_ref, left_ref, far0_ref, far1_ref, right_out, left_out):
    right_out[...] = (right_ref[...].astype(F32) + far0_ref[...].astype(F32)).astype(BF)
    left_out[...] = (left_ref[...].astype(F32) + far1_ref[...].astype(F32)).astype(BF)


def middle(to_right, to_left, far0, far1):
    width = far0.shape[1]
    return pl.pallas_call(
        middle_kernel,
        grid=(1,),
        out_shape=(jax.ShapeDtypeStruct((128, width), BF),) * 2,
        in_specs=[
            pl.BlockSpec((64, width), lambda i: (0, 0)),
            pl.BlockSpec((64, width), lambda i: (1, 0)),
            pl.BlockSpec((64, width), lambda i: (0, 0)),
            pl.BlockSpec((64, width), lambda i: (0, 0)),
        ],
        out_specs=(
            pl.BlockSpec((64, width), lambda i: (0, 0)),
            pl.BlockSpec((64, width), lambda i: (1, 0)),
        ),
        input_output_aliases={0: 0, 1: 1},
        compiler_params=PARAMS,
        cost_estimate=cost(128 * width, 6 * 64 * width * 2),
        name="middle",
    )(to_right, to_left, far0, far1)


def total_kernel(own0, lft0, rgt0, own1, lft1, rgt1, out_ref):
    for part, (own, lft, rgt) in enumerate(((own0, lft0, rgt0), (own1, lft1, rgt1))):
        value = own[...].astype(F32) + lft[...].astype(F32) + rgt[...].astype(F32)
        out_ref[pl.ds(part * 128, 128), :] = value.astype(BF)


def total(parts):
    width = parts[0].shape[1]
    return pl.pallas_call(
        total_kernel,
        out_shape=jax.ShapeDtypeStruct((256, width), BF),
        in_specs=[VMEM] * 6,
        out_specs=VMEM,
        compiler_params=PARAMS,
        cost_estimate=cost(4 * 128 * width, 8 * 128 * width * 2),
        name="total",
    )(*parts)


def finish_kernel(back_ref, expert_ref, slot_ref, out_ref):
    sums = []
    for core in range(2):
        pair = [back_ref[pl.ds(core * 128 + z * 64, 64), :].astype(F32) for z in range(2)]
        sums.append((pair[0] + pair[1]).astype(BF))
    returned = jnp.concatenate(sums, axis=0)
    placing = placing_of(expert_ref[...], slot_ref[...])
    out_ref[...] = dot(returned, placing, 0, 0).astype(BF)


def finish(back, expert, slot):
    width = back.shape[1]
    return pl.pallas_call(
        finish_kernel,
        out_shape=jax.ShapeDtypeStruct((width, 128), BF),
        in_specs=[VMEM] * 3,
        out_specs=VMEM,
        compiler_params=PARAMS,
        cost_estimate=cost(2 * 128 * 128 * width, 3 * 128 * width * 2),
        name="finish",
    )(back, expert, slot)


def weights_kernel(a0, b0, a1, b1, out_ref):
    value = dot(a0[...], b0[...], 0, 0) + dot(a1[...], b1[...], 0, 0)
    out_ref[...] = value.astype(BF)


def weights(a, b, a_part, b_part):
    width, units = a[0].shape[1], b[0].shape[1]
    spec_a = [pl.BlockSpec((512, 256), lambda i, p=p: (p, i)) for p in a_part]
    spec_b = [pl.BlockSpec((512, units), lambda i, p=p: (p, 0)) for p in b_part]
    return pl.pallas_call(
        weights_kernel,
        grid=(pl.cdiv(width, 256),),
        out_shape=jax.ShapeDtypeStruct((width, units), BF),
        in_specs=[spec_a[0], spec_b[0], spec_a[1], spec_b[1]],
        out_specs=pl.BlockSpec((256, units), lambda i: (i, 0)),
        compiler_params=PARAMS,
        cost_estimate=cost(2 * 1024 * width * units, 10 << 20),
        name="weights",
    )(a[0], b[0], a[1], b[1])


def move(value, axis, pairs):
    blocks = value.reshape(-1, 64, value.shape[1])
    return lax.ppermute(blocks, axis, pairs).reshape(value.shape)


def right(value):
    return move(value, "x", RIGHT)


def left(value):
    return move(value, "x", LEFT)


def other_z(value):
    return move(value, "zl", SWAP)


def exchange(value):
    blocks = value.reshape(32, 8, value.shape[1])
    return lax.all_to_all(blocks, EXCHANGE, split_axis=0, concat_axis=0, tiled=True).reshape(value.shape)


def gather_x(own):
    from_left = right(own)
    from_right = left(own)
    return [own, from_left, from_right, right(from_left[:64]), left(from_right[64:])]


def per_device(grad_out, expert_id, slot, gate_prob, saved_inputs, w_in, w_out):
    width = grad_out.shape[1]
    z = lax.axis_index("zl").astype(jnp.int32).reshape(1)
    expert = expert_id.reshape(1, -1)
    place = slot.reshape(1, -1)
    first = w_in[0]
    second = w_out[0].T

    outgoing, own = prepare(grad_out.T, expert, place, gate_prob.reshape(1, -1), saved_inputs[0].reshape(128, width))
    arrived = exchange(outgoing)
    near = gather_x(own)
    far = [other_z(piece) for piece in near]
    cotangents = [gather_x(arrived[part * 128 : part * 128 + 128]) for part in range(2)]

    rows, hidden, slope = forward(z, near + far, first)
    grads = []
    dhiddens = []
    summands = []
    for part in range(2):
        g_rows, dhidden, pown, plft, prgt, pfar0, pfar1 = backward(part, cotangents[part], slope, second, first)
        grads.append(g_rows)
        dhiddens.append(dhidden)
        to_right, to_left = middle(prgt, plft, right(pfar0), left(pfar1))
        summands += [pown, right(to_right), left(to_left)]
    came_back = exchange(total(summands))
    grad_in = weights((rows, rows), dhiddens, (0, 1), (0, 0))
    grad_out_w = weights(grads, (hidden, hidden), (0, 0), (0, 1))
    tokens = finish(came_back, expert, place)
    return (tokens.T, grad_in[None], grad_out_w.T[None])


def solution(mesh):
    fine = Mesh(mesh.devices.reshape(4, 2, 2, 4, 2), AXES)
    wide = ("y", "zh", "core")
    local = ("x", "zl")
    placed = (
        P(wide + local, None),
        P(wide + local),
        P(wide + local),
        P(wide + local),
        P(wide, None, local, None),
        P(wide, None, local),
        P(wide, local, None),
    )
    return jax.shard_map(
        per_device,
        mesh=fine,
        in_specs=placed,
        out_specs=(P(wide + local, None), P(wide, None, local), P(wide, local, None)),
        check_vma=False,
    )
```

```python
import jax
import jax.numpy as jnp
from jax import lax
from jax.experimental import pallas as pl
from jax.experimental.pallas import tpu as pltpu
from jax.sharding import Mesh, PartitionSpec as P

AXES = ("y", "zh", "core", "x", "zl")
WIDE = ("y", "zh", "core")
LOCAL = ("x", "zl")
WIDE_AND_Z = ("zl",) + WIDE
RIGHT = [(i, (i + 1) % 4) for i in range(4)]
LEFT = [(i, (i - 1) % 4) for i in range(4)]
ACROSS = [(i, (i + 2) % 4) for i in range(4)]
SWAP = [(0, 1), (1, 0)]
BF = jnp.bfloat16
F32 = jnp.float32
VMEM = pl.BlockSpec(memory_space=pltpu.VMEM)
ANY = pl.BlockSpec(memory_space=pl.ANY)
SMEM = pl.BlockSpec(memory_space=pltpu.SMEM)
PARAMS = pltpu.CompilerParams(vmem_limit_bytes=24 * 1024 * 1024)


def dot(a, b, da, db):
    return lax.dot_general(a, b, (((da,), (db,)), ((), ())), preferred_element_type=F32)


def call(kernel, outs, args, name, after=()):
    def ordered(*refs):
        kernel(*refs[: len(args)], *refs[len(args) + len(after) :])

    return pl.pallas_call(
        ordered,
        out_shape=tuple(jax.ShapeDtypeStruct(s, d) for s, d in outs),
        in_specs=[VMEM] * len(args) + [ANY] * len(after),
        out_specs=(VMEM,) * len(outs),
        compiler_params=PARAMS,
        cost_estimate=pl.CostEstimate(flops=0, bytes_accessed=0, transcendentals=0),
        name=name,
    )(*args, *after)


def stacked(refs):
    return jnp.concatenate([ref[...] for ref in refs], axis=0)


def placing_of(expert, slot):
    target = jnp.where(slot >= 0, expert * 8 + slot, -1)
    rows = lax.broadcasted_iota(jnp.int32, (128, 128), 0)
    return jnp.where(rows == target, 1.0, 0.0).astype(BF)


def prepare_kernel(grad, expert, slot, gate, out_ref, grad_ref, expert_ref, slot_ref, gate_ref, sems):
    pairs = ((grad, grad_ref), (expert, expert_ref), (slot, slot_ref), (gate, gate_ref))
    copies = [pltpu.make_async_copy(src, dst, sems.at[i]) for i, (src, dst) in enumerate(pairs)]
    for copy in copies:
        copy.start()
    for copy in copies:
        copy.wait()
    scaled = (gate_ref[...] * grad_ref[...].astype(F32)).astype(BF)
    outgoing = dot(placing_of(expert_ref[...], slot_ref[...]), scaled, 1, 1).astype(BF)
    out_ref[...] = outgoing


def prepare(*args):
    width = args[0].shape[0]
    args = [pltpu.with_memory_space_constraint(a, pltpu.HBM) for a in args]
    return pl.pallas_call(
        prepare_kernel,
        out_shape=jax.ShapeDtypeStruct((128, width), BF),
        in_specs=[pl.BlockSpec(memory_space=pltpu.HBM)] * 4,
        out_specs=VMEM,
        scratch_shapes=[pltpu.VMEM(a.shape, a.dtype) for a in args] + [pltpu.SemaphoreType.DMA((4,))],
        compiler_params=PARAMS,
        cost_estimate=pl.CostEstimate(
            flops=2 * 128 * 128 * width, bytes_accessed=8 * 128 * width, transcendentals=0
        ),
        name="prepare",
    )(*args)


def gelu_parts(value):
    normal_cdf = 0.5 * (1.0 + lax.erf(value * 0.7071067811865476))
    density = jnp.exp(-0.5 * value * value) * 0.3989422804014327
    return value * normal_cdf, normal_cdf + value * density


def forward_kernel(own, lft, rgt, far, w_ref, hidden_ref, slope_ref):
    pre = dot(stacked((own, lft, rgt, far)), w_ref[...], 1, 0)
    value, slope = gelu_parts(pre)
    hidden_ref[...] = value.astype(BF)
    slope_ref[...] = slope


def forward(pieces, w_in, after=()):
    units = w_in.shape[1]
    outs = (((512, units), BF), ((512, units), F32))
    return call(forward_kernel, outs, (*pieces, w_in), "forward", after)


def backward_kernel(own, lft, rgt, far, slope_ref, wo_ref, wi_ref, dhidden_ref, *outs):
    back = dot(stacked((own, lft, rgt, far)), wo_ref[...], 1, 0)
    dhidden = (back * slope_ref[...]).astype(BF)
    dhidden_ref[...] = dhidden
    partial_value = dot(dhidden, wi_ref[...], 1, 1).astype(BF)
    start = 0
    for out in outs:
        size = out.shape[0]
        out[...] = partial_value[start : start + size]
        start += size


def backward(pieces, slope, w_out_t, w_in, after=()):
    width, units = w_in.shape
    outs = (((512, units), BF),) + (((128, width), BF),) * 3 + (((64, width), BF),) * 2
    args = (*pieces, slope, w_out_t, w_in)
    dhidden, *partials = call(backward_kernel, outs, args, "backward", after)
    return dhidden, partials


def middle_kernel(rgt, lft, far0, far1, rgt_out, lft_out):
    top, low = pl.ds(0, 64), pl.ds(64, 64)
    rgt_out[top, :] = (rgt[top, :].astype(F32) + far0[...].astype(F32)).astype(BF)
    rgt_out[low, :] = rgt[low, :]
    lft_out[top, :] = lft[top, :]
    lft_out[low, :] = (lft[low, :].astype(F32) + far1[...].astype(F32)).astype(BF)


def reduce_x(partials):
    own, lft, rgt, from_left, from_right = partials
    outs = ((rgt.shape, BF),) * 2
    rgt, lft = call(middle_kernel, outs, (rgt, lft, from_left, from_right), "middle")
    return own, right(rgt), left(lft)


def nothing(*refs):
    pass


def after(value, *others):
    return pl.pallas_call(
        nothing,
        out_shape=jax.ShapeDtypeStruct(value.shape, value.dtype),
        in_specs=[ANY] * (1 + len(others)),
        out_specs=ANY,
        input_output_aliases={0: 0},
        compiler_params=PARAMS,
        cost_estimate=pl.CostEstimate(flops=0, bytes_accessed=0, transcendentals=0),
        name="after",
    )(value, *others)


def total_kernel(z_ref, *refs):
    out_ref = refs[-1]
    for i, start in enumerate((z_ref[0] * 128, (1 - z_ref[0]) * 128)):
        value = sum(ref[...].astype(F32) for ref in refs[3 * i : 3 * i + 3])
        out_ref[pl.ds(pl.multiple_of(start, 128), 128), :] = value.astype(BF)


def total(z, near, far, later):
    width = near[0].shape[1]
    return pl.pallas_call(
        total_kernel,
        out_shape=jax.ShapeDtypeStruct((256, width), BF),
        in_specs=[SMEM] + [VMEM] * 6 + [ANY] * len(later),
        out_specs=VMEM,
        compiler_params=PARAMS,
        cost_estimate=pl.CostEstimate(flops=0, bytes_accessed=0, transcendentals=0),
        name="total",
    )(z, *near, *far, *later)


def finish_kernel(back_ref, expert_ref, slot_ref, out_ref):
    returned = (back_ref[:128, :].astype(F32) + back_ref[128:, :].astype(F32)).astype(BF)
    out_ref[...] = dot(returned, placing_of(expert_ref[...], slot_ref[...]), 0, 0).astype(BF)


def finish(back, expert, slot):
    width = back.shape[1]
    outs = (((width, 128), BF),)
    return call(finish_kernel, outs, (back, expert, slot), "finish")[0]


def weights_kernel(*refs):
    pieces, b0, b1, out, rows, b, blocks, sems, b_sems, out_sems = refs[:8], *refs[8:]
    width = out.shape[0]
    cut = 1024
    loads = []
    for part, at in enumerate((pl.ds(0, cut), pl.ds(cut, width - cut))):
        loads.append(
            [
                pltpu.make_async_copy(piece.at[:, at], rows.at[pl.ds(i * 128, 128), at], sems.at[part * 8 + i])
                for i, piece in enumerate(pieces)
            ]
        )
    loads[0] += [
        pltpu.make_async_copy(half, b.at[pl.ds(i * 512, 512), :], b_sems.at[i]) for i, half in enumerate((b0, b1))
    ]
    for part in loads:
        for copy in part:
            copy.start()
    writes = []
    for i, start in enumerate(range(0, width, 256)):
        if start in (0, cut):
            for copy in loads[start // cut]:
                copy.wait()
        size = min(256, width - start)
        if i >= 2:
            writes[i - 2].wait()
        block = blocks.at[i % 2, pl.ds(0, size), :]
        block[...] = dot(rows[:, pl.ds(start, size)], b[...], 0, 0).astype(BF)
        writes.append(pltpu.make_async_copy(block, out.at[pl.ds(start, size), :], out_sems.at[i % 2]))
        writes[i].start()
    for write in writes[-2:]:
        write.wait()


def weights(pieces, b0, b1):
    width, units = pieces[0].shape[1], b0.shape[1]
    args = [pltpu.with_memory_space_constraint(a, pltpu.HBM) for a in (*pieces, b0, b1)]
    return pl.pallas_call(
        weights_kernel,
        out_shape=pltpu.HBM((width, units), BF),
        in_specs=[pl.BlockSpec(memory_space=pltpu.HBM)] * 10,
        out_specs=pl.BlockSpec(memory_space=pltpu.HBM),
        scratch_shapes=[
            pltpu.VMEM((1024, width), BF),
            pltpu.VMEM((1024, units), BF),
            pltpu.VMEM((2, 256, units), BF),
            pltpu.SemaphoreType.DMA((16,)),
            pltpu.SemaphoreType.DMA((2,)),
            pltpu.SemaphoreType.DMA((2,)),
        ],
        compiler_params=PARAMS,
        cost_estimate=pl.CostEstimate(
            flops=2 * 1024 * width * units, bytes_accessed=10 << 20, transcendentals=0
        ),
        name="weights",
    )(*args)


def move(value, axis, pairs):
    blocks = value.reshape(-1, 64, value.shape[1])
    return lax.ppermute(blocks, axis, pairs).reshape(value.shape)


def right(value):
    return move(value, "x", RIGHT)


def left(value):
    return move(value, "x", LEFT)


def opposite(value):
    return move(value, "x", ACROSS)


def other_z(value):
    return move(value, "zl", SWAP)


def exchange(value, axes):
    blocks = value.reshape(-1, 8, value.shape[1])
    return lax.all_to_all(blocks, axes, split_axis=0, concat_axis=0, tiled=True).reshape(value.shape)


def per_device(grad_out, expert_id, slot, gate_prob, saved_inputs, w_in, w_out):
    width = grad_out.shape[1]
    expert = expert_id.reshape(1, -1)
    place = slot.reshape(1, -1)
    first = w_in[0]
    second = w_out[0].T
    z = lax.axis_index("zl").astype(jnp.int32).reshape(1)

    x_own = saved_inputs[0].reshape(128, width)
    x_lft, x_rgt, x_far, xz_own = right(x_own), left(x_own), opposite(x_own), other_z(x_own)
    g_own = exchange(prepare(grad_out.T, expert, place, gate_prob.reshape(1, -1)), WIDE)
    g_own = after(g_own, x_lft, x_rgt, x_far, xz_own)

    g_lft, g_rgt, gz_own = right(g_own), left(g_own), other_z(g_own)
    xz_lft = other_z(x_lft)

    gz_own = after(gz_own, g_lft, g_rgt)
    gz_lft, g_far, xz_rgt = right(gz_own), left(g_rgt), other_z(x_rgt)
    hidden, slope = forward((x_own, x_lft, x_rgt, x_far), first)

    gz_lft = after(gz_lft, g_far, xz_lft)
    gz_own = after(gz_own, gz_lft)
    gz_far, gz_rgt, xz_far = right(gz_lft), left(gz_own), other_z(x_far)
    dhidden, (*partials, far0, far1) = backward((g_own, g_lft, g_rgt, g_far), slope, second, first)
    arrived = right(far0), left(far1)
    summands = reduce_x((*partials, *arrived))

    hidden_z, slope_z = forward((xz_own, xz_lft, xz_rgt, xz_far), first, arrived)
    dhidden_z, (*partials_z, far0, far1) = backward((gz_own, gz_lft, gz_rgt, gz_far), slope_z, second, first)
    summands_z = reduce_x((*partials_z, right(far0), left(far1)))
    grad_out_w = weights((g_own, g_lft, g_rgt, g_far, gz_own, gz_lft, gz_rgt, gz_far), hidden, hidden_z)
    grad_in = weights((x_own, x_lft, x_rgt, x_far, xz_own, xz_lft, xz_rgt, xz_far), dhidden, dhidden_z)
    came_back = exchange(total(z, summands, summands_z, ()), WIDE_AND_Z)
    tokens = finish(came_back, expert, place)
    return (tokens.T, grad_in[None], grad_out_w.T[None])


def solution(mesh):
    fine = Mesh(mesh.devices.reshape(4, 2, 2, 4, 2), AXES)
    every = WIDE + LOCAL
    placed = (
        P(every, None),
        P(every),
        P(every),
        P(every),
        P(WIDE, None, LOCAL, None),
        P(WIDE, None, LOCAL),
        P(WIDE, LOCAL, None),
    )
    return jax.shard_map(
        per_device,
        mesh=fine,
        in_specs=placed,
        out_specs=(P(every, None), P(WIDE, None, LOCAL), P(WIDE, LOCAL, None)),
        check_vma=False,
    )
```

```python
import functools

import jax
import jax.numpy as jnp
from jax import lax
from jax.experimental import pallas as pl
from jax.experimental.pallas import tpu as pltpu
from jax.sharding import Mesh, PartitionSpec as P

AXES = ("y", "zh", "core", "x", "zl")
WIDE = ("y", "zh", "core")
LOCAL = ("x", "zl")
WIDE_AND_Z = ("zl",) + WIDE
RIGHT = [(i, (i + 1) % 4) for i in range(4)]
LEFT = [(i, (i - 1) % 4) for i in range(4)]
ACROSS = [(i, (i + 2) % 4) for i in range(4)]
SWAP = [(0, 1), (1, 0)]
BF = jnp.bfloat16
F32 = jnp.float32
VMEM = pl.BlockSpec(memory_space=pltpu.VMEM)
ANY = pl.BlockSpec(memory_space=pl.ANY)
SMEM = pl.BlockSpec(memory_space=pltpu.SMEM)
PARAMS = pltpu.CompilerParams(vmem_limit_bytes=24 * 1024 * 1024)


def dot(a, b, da, db):
    return lax.dot_general(a, b, (((da,), (db,)), ((), ())), preferred_element_type=F32)


def call(kernel, outs, args, name, after=()):
    def ordered(*refs):
        kernel(*refs[: len(args)], *refs[len(args) + len(after) :])

    return pl.pallas_call(
        ordered,
        out_shape=tuple(jax.ShapeDtypeStruct(s, d) for s, d in outs),
        in_specs=[VMEM] * len(args) + [ANY] * len(after),
        out_specs=(VMEM,) * len(outs),
        compiler_params=PARAMS,
        cost_estimate=pl.CostEstimate(flops=0, bytes_accessed=0, transcendentals=0),
        name=name,
    )(*args, *after)


def stacked(refs):
    return jnp.concatenate([ref[...] for ref in refs], axis=0)


def placing_of(expert, slot):
    target = jnp.where(slot >= 0, expert * 8 + slot, -1)
    rows = lax.broadcasted_iota(jnp.int32, (128, 128), 0)
    return jnp.where(rows == target, 1.0, 0.0).astype(BF)


def prepare_kernel(grad, expert, slot, gate, out_ref, grad_ref, expert_ref, slot_ref, gate_ref, sems):
    pairs = ((grad, grad_ref), (expert, expert_ref), (slot, slot_ref), (gate, gate_ref))
    copies = [pltpu.make_async_copy(src, dst, sems.at[i]) for i, (src, dst) in enumerate(pairs)]
    for copy in copies:
        copy.start()
    for copy in copies:
        copy.wait()
    scaled = (gate_ref[...] * grad_ref[...].astype(F32)).astype(BF)
    outgoing = dot(placing_of(expert_ref[...], slot_ref[...]), scaled, 1, 1).astype(BF)
    out_ref[...] = outgoing


def prepare(*args):
    width = args[0].shape[0]
    args = [pltpu.with_memory_space_constraint(a, pltpu.HBM) for a in args]
    return pl.pallas_call(
        prepare_kernel,
        out_shape=jax.ShapeDtypeStruct((128, width), BF),
        in_specs=[pl.BlockSpec(memory_space=pltpu.HBM)] * 4,
        out_specs=VMEM,
        scratch_shapes=[pltpu.VMEM(a.shape, a.dtype) for a in args] + [pltpu.SemaphoreType.DMA((4,))],
        compiler_params=PARAMS,
        cost_estimate=pl.CostEstimate(
            flops=2 * 128 * 128 * width, bytes_accessed=8 * 128 * width, transcendentals=0
        ),
        name="prepare",
    )(*args)


def gelu_parts(value):
    normal_cdf = 0.5 * (1.0 + lax.erf(value * 0.7071067811865476))
    density = jnp.exp(-0.5 * value * value) * 0.3989422804014327
    return value * normal_cdf, normal_cdf + value * density


def layer_kernel(count, *refs):
    x, g = refs[:count], refs[count : 2 * count]
    wi_ref, wo_ref, hidden_ref, dhidden_ref, *outs = refs[2 * count :]
    value, slope = gelu_parts(dot(stacked(x), wi_ref[...], 1, 0))
    hidden_ref[...] = value.astype(BF)
    dhidden = (dot(stacked(g), wo_ref[...], 1, 0) * slope).astype(BF)
    dhidden_ref[...] = dhidden
    partial_value = dot(dhidden, wi_ref[...], 1, 1).astype(BF)
    start = 0
    for out in outs:
        size = out.shape[0]
        out[...] = partial_value[start : start + size]
        start += size


def layer(x, g, w_in, w_out_t, sizes, before=()):
    width, units = w_in.shape
    rows = 128 * len(x)
    outs = (((rows, units), BF),) * 2 + tuple(((size, width), BF) for size in sizes)
    kernel = functools.partial(layer_kernel, len(x))
    hidden, dhidden, *partials = call(kernel, outs, (*x, *g, w_in, w_out_t), "layer", before)
    return hidden, dhidden, partials


def middle_kernel(rgt, lft, far0, far1, rgt_out, lft_out):
    rgt_out[...] = (rgt[...].astype(F32) + far0[...].astype(F32)).astype(BF)
    lft_out[...] = (lft[...].astype(F32) + far1[...].astype(F32)).astype(BF)


def middle(rgt, lft, from_left, from_right, before=()):
    return call(middle_kernel, ((rgt.shape, BF),) * 2, (rgt, lft, from_left, from_right), "middle", before)


def nothing(*refs):
    pass


def after(value, *others):
    return pl.pallas_call(
        nothing,
        out_shape=jax.ShapeDtypeStruct(value.shape, value.dtype),
        in_specs=[ANY] * (1 + len(others)),
        out_specs=ANY,
        input_output_aliases={0: 0},
        compiler_params=PARAMS,
        cost_estimate=pl.CostEstimate(flops=0, bytes_accessed=0, transcendentals=0),
        name="after",
    )(value, *others)


def total_kernel(z_ref, *refs):
    out_ref = refs[-1]
    for i, start in enumerate((z_ref[0] * 128, (1 - z_ref[0]) * 128)):
        own, *halves = refs[5 * i : 5 * i + 5]
        for half in range(2):
            value = own[pl.ds(half * 64, 64), :].astype(F32)
            for ref in halves[half::2]:
                value = value + ref[...].astype(F32)
            out_ref[pl.ds(pl.multiple_of(start + half * 64, 64), 64), :] = value.astype(BF)


def total(z, near, far):
    width = near[0].shape[1]
    return pl.pallas_call(
        total_kernel,
        out_shape=jax.ShapeDtypeStruct((256, width), BF),
        in_specs=[SMEM] + [VMEM] * 10,
        out_specs=VMEM,
        compiler_params=PARAMS,
        cost_estimate=pl.CostEstimate(flops=0, bytes_accessed=0, transcendentals=0),
        name="total",
    )(z, *near, *far)


def finish_kernel(back_ref, expert_ref, slot_ref, out_ref):
    returned = (back_ref[:128, :].astype(F32) + back_ref[128:, :].astype(F32)).astype(BF)
    out_ref[...] = dot(returned, placing_of(expert_ref[...], slot_ref[...]), 0, 0).astype(BF)


def finish(back, expert, slot):
    width = back.shape[1]
    outs = (((width, 128), BF),)
    return call(finish_kernel, outs, (back, expert, slot), "finish")[0]


def weights_kernel(*refs):
    pieces, factors = refs[:8], refs[8:12]
    out, rows, b, blocks, sems, b_sems, out_sems = refs[12:]
    width = out.shape[0]
    cut = 1024
    loads = []
    for part, at in enumerate((pl.ds(0, cut), pl.ds(cut, width - cut))):
        loads.append(
            [
                pltpu.make_async_copy(piece.at[:, at], rows.at[pl.ds(i * 128, 128), at], sems.at[part * 8 + i])
                for i, piece in enumerate(pieces)
            ]
        )
    loads[0] += [
        pltpu.make_async_copy(factor, b.at[pl.ds(start, factor.shape[0]), :], b_sems.at[i])
        for i, (factor, start) in enumerate(zip(factors, (0, 384, 512, 896)))
    ]
    for part in loads:
        for copy in part:
            copy.start()
    writes = []
    for i, start in enumerate(range(0, width, 256)):
        if start in (0, cut):
            for copy in loads[start // cut]:
                copy.wait()
        size = min(256, width - start)
        if i >= 2:
            writes[i - 2].wait()
        block = blocks.at[i % 2, pl.ds(0, size), :]
        block[...] = dot(rows[:, pl.ds(start, size)], b[...], 0, 0).astype(BF)
        writes.append(pltpu.make_async_copy(block, out.at[pl.ds(start, size), :], out_sems.at[i % 2]))
        writes[i].start()
    for write in writes[-2:]:
        write.wait()


def weights(pieces, factors):
    width, units = pieces[0].shape[1], factors[0].shape[1]
    args = [pltpu.with_memory_space_constraint(a, pltpu.HBM) for a in (*pieces, *factors)]
    return pl.pallas_call(
        weights_kernel,
        out_shape=pltpu.HBM((width, units), BF),
        in_specs=[pl.BlockSpec(memory_space=pltpu.HBM)] * 12,
        out_specs=pl.BlockSpec(memory_space=pltpu.HBM),
        scratch_shapes=[
            pltpu.VMEM((1024, width), BF),
            pltpu.VMEM((1024, units), BF),
            pltpu.VMEM((2, 256, units), BF),
            pltpu.SemaphoreType.DMA((16,)),
            pltpu.SemaphoreType.DMA((4,)),
            pltpu.SemaphoreType.DMA((2,)),
        ],
        compiler_params=PARAMS,
        cost_estimate=pl.CostEstimate(
            flops=2 * 1024 * width * units, bytes_accessed=10 << 20, transcendentals=0
        ),
        name="weights",
    )(*args)


def move(value, axis, pairs):
    blocks = value.reshape(-1, 64, value.shape[1])
    return lax.ppermute(blocks, axis, pairs).reshape(value.shape)


def right(value):
    return move(value, "x", RIGHT)


def left(value):
    return move(value, "x", LEFT)


def opposite(value):
    return move(value, "x", ACROSS)


def other_z(value):
    return move(value, "zl", SWAP)


def exchange(value, axes):
    blocks = value.reshape(-1, 8, value.shape[1])
    return lax.all_to_all(blocks, axes, split_axis=0, concat_axis=0, tiled=True).reshape(value.shape)


def per_device(grad_out, expert_id, slot, gate_prob, saved_inputs, w_in, w_out):
    width = grad_out.shape[1]
    expert = expert_id.reshape(1, -1)
    place = slot.reshape(1, -1)
    first = w_in[0]
    second = w_out[0].T
    z = lax.axis_index("zl").astype(jnp.int32).reshape(1)

    x_own = saved_inputs[0].reshape(128, width)
    x_lft, x_rgt, x_far, xz_own = right(x_own), left(x_own), opposite(x_own), other_z(x_own)
    g_own = exchange(prepare(grad_out.T, expert, place, gate_prob.reshape(1, -1)), WIDE)
    g_own = after(g_own, x_lft, x_rgt, x_far, xz_own)

    g_lft, g_rgt, gz_own = right(g_own), left(g_own), other_z(g_own)
    xz_lft = other_z(x_lft)

    gz_own = after(gz_own, g_lft, g_rgt)
    gz_lft, g_far, xz_far = right(gz_own), left(g_rgt), other_z(x_far)
    hidden_b, dhidden_b, partials = layer(
        (x_own, x_lft, x_rgt), (g_own, g_lft, g_rgt), first, second, (128, 64, 64, 64, 64)
    )

    gz_lft = after(gz_lft, g_far)
    gz_own = after(gz_own, gz_lft)
    gz_far, gz_rgt, xz_rgt = right(gz_lft), left(gz_own), other_z(x_rgt)
    p_own, lft0, lft1, rgt0, rgt1 = partials
    s_lft1, s_rgt0 = right(rgt1), left(lft0)
    hidden_a, dhidden_a, (far0, far1) = layer((x_far,), (g_far,), first, second, (64, 64), (s_lft1, s_rgt0))
    rgt0, lft1 = middle(rgt0, lft1, right(far0), left(far1), (xz_far, xz_lft))
    summands = p_own, right(rgt0), s_lft1, s_rgt0, left(lft1)

    hidden_az, dhidden_az, (far0, far1) = layer((xz_far,), (gz_far,), first, second, (64, 64), (rgt0, gz_rgt))
    hidden_bz, dhidden_bz, partials_z = layer(
        (xz_own, xz_lft, xz_rgt), (gz_own, gz_lft, gz_rgt), first, second, (128, 64, 64, 64, 64), (dhidden_az,)
    )
    pz_own, lft0, lft1, rgt0, rgt1 = partials_z
    s_lft1, s_rgt0 = right(rgt1), left(lft0)
    rgt0, lft1 = middle(rgt0, lft1, right(far0), left(far1), summands[1:])
    summands_z = pz_own, right(rgt0), s_lft1, s_rgt0, left(lft1)
    g_all = (g_own, g_lft, g_rgt, g_far, gz_own, gz_lft, gz_rgt, gz_far)
    x_all = (x_own, x_lft, x_rgt, x_far, xz_own, xz_lft, xz_rgt, xz_far)
    grad_out_w = weights(g_all, (hidden_b, hidden_a, hidden_bz, hidden_az))
    grad_in = weights(x_all, (dhidden_b, dhidden_a, dhidden_bz, dhidden_az))
    came_back = exchange(total(z, summands, summands_z), WIDE_AND_Z)
    tokens = finish(came_back, expert, place)
    return (tokens.T, grad_in[None], grad_out_w.T[None])


def solution(mesh):
    fine = Mesh(mesh.devices.reshape(4, 2, 2, 4, 2), AXES)
    every = WIDE + LOCAL
    placed = (
        P(every, None),
        P(every),
        P(every),
        P(every),
        P(WIDE, None, LOCAL, None),
        P(WIDE, None, LOCAL),
        P(WIDE, LOCAL, None),
    )
    return jax.shard_map(
        per_device,
        mesh=fine,
        in_specs=placed,
        out_specs=(P(every, None), P(WIDE, None, LOCAL), P(WIDE, LOCAL, None)),
        check_vma=False,
    )
```

```python
import functools

import jax
import jax.numpy as jnp
from jax import lax
from jax.experimental import pallas as pl
from jax.experimental.pallas import tpu as pltpu
from jax.sharding import Mesh, PartitionSpec as P

AXES = ("y", "zh", "core", "x", "zl")
WIDE = ("y", "zh", "core")
LOCAL = ("x", "zl")
WIDE_AND_Z = ("zl",) + WIDE
RIGHT = [(i, (i + 1) % 4) for i in range(4)]
LEFT = [(i, (i - 1) % 4) for i in range(4)]
ACROSS = [(i, (i + 2) % 4) for i in range(4)]
SWAP = [(0, 1), (1, 0)]
BF = jnp.bfloat16
F32 = jnp.float32
VMEM = pl.BlockSpec(memory_space=pltpu.VMEM)
ANY = pl.BlockSpec(memory_space=pl.ANY)
SMEM = pl.BlockSpec(memory_space=pltpu.SMEM)
PARAMS = pltpu.CompilerParams(vmem_limit_bytes=14 * 1024 * 1024)


def dot(a, b, da, db):
    return lax.dot_general(a, b, (((da,), (db,)), ((), ())), preferred_element_type=F32)


def call(kernel, outs, args, name, after=()):
    def ordered(*refs):
        kernel(*refs[: len(args)], *refs[len(args) + len(after) :])

    return pl.pallas_call(
        ordered,
        out_shape=tuple(jax.ShapeDtypeStruct(s, d) for s, d in outs),
        in_specs=[VMEM] * len(args) + [ANY] * len(after),
        out_specs=(VMEM,) * len(outs),
        compiler_params=PARAMS,
        cost_estimate=pl.CostEstimate(flops=0, bytes_accessed=0, transcendentals=0),
        name=name,
    )(*args, *after)


def stacked(refs):
    return jnp.concatenate([ref[...] for ref in refs], axis=0)


def placing_of(expert, slot):
    target = jnp.where(slot >= 0, expert * 8 + slot, -1)
    rows = lax.broadcasted_iota(jnp.int32, (128, 128), 0)
    return jnp.where(rows == target, 1.0, 0.0).astype(BF)


def prepare_kernel(grad, expert, slot, gate, out_ref, grad_ref, expert_ref, slot_ref, gate_ref, sems):
    pairs = ((grad, grad_ref), (expert, expert_ref), (slot, slot_ref), (gate, gate_ref))
    copies = [pltpu.make_async_copy(src, dst, sems.at[i]) for i, (src, dst) in enumerate(pairs)]
    for copy in copies:
        copy.start()
    for copy in copies:
        copy.wait()
    scaled = (gate_ref[...] * grad_ref[...].astype(F32)).astype(BF)
    outgoing = dot(placing_of(expert_ref[...], slot_ref[...]), scaled, 1, 1).astype(BF)
    out_ref[...] = outgoing


def prepare(*args):
    width = args[0].shape[0]
    args = [pltpu.with_memory_space_constraint(a, pltpu.HBM) for a in args]
    return pl.pallas_call(
        prepare_kernel,
        out_shape=jax.ShapeDtypeStruct((128, width), BF),
        in_specs=[pl.BlockSpec(memory_space=pltpu.HBM)] * 4,
        out_specs=VMEM,
        scratch_shapes=[pltpu.VMEM(a.shape, a.dtype) for a in args] + [pltpu.SemaphoreType.DMA((4,))],
        compiler_params=PARAMS,
        cost_estimate=pl.CostEstimate(
            flops=2 * 128 * 128 * width, bytes_accessed=8 * 128 * width, transcendentals=0
        ),
        name="prepare",
    )(*args)


def gelu_parts(value):
    normal_cdf = 0.5 * (1.0 + lax.erf(value * 0.7071067811865476))
    density = jnp.exp(-0.5 * value * value) * 0.3989422804014327
    return value * normal_cdf, normal_cdf + value * density


def layer_kernel(count, *refs):
    x, g = refs[:count], refs[count : 2 * count]
    wi_ref, wo_ref, hidden_ref, dhidden_ref, *outs = refs[2 * count :]
    value, slope = gelu_parts(dot(stacked(x), wi_ref[...], 1, 0))
    hidden_ref[...] = value.astype(BF)
    dhidden = (dot(stacked(g), wo_ref[...], 1, 0) * slope).astype(BF)
    dhidden_ref[...] = dhidden
    partial_value = dot(dhidden, wi_ref[...], 1, 1).astype(BF)
    start = 0
    for out in outs:
        size = out.shape[0]
        out[...] = partial_value[start : start + size]
        start += size


def layer(x, g, w_in, w_out_t, sizes, before=()):
    width, units = w_in.shape
    rows = 128 * len(x)
    outs = (((rows, units), BF),) * 2 + tuple(((size, width), BF) for size in sizes)
    kernel = functools.partial(layer_kernel, len(x))
    hidden, dhidden, *partials = call(kernel, outs, (*x, *g, w_in, w_out_t), "layer", before)
    return hidden, dhidden, partials


def middle_kernel(rgt, lft, far0, far1, rgt_out, lft_out):
    rgt_out[...] = (rgt[...].astype(F32) + far0[...].astype(F32)).astype(BF)
    lft_out[...] = (lft[...].astype(F32) + far1[...].astype(F32)).astype(BF)


def middle(rgt, lft, from_left, from_right, before=()):
    return call(middle_kernel, ((rgt.shape, BF),) * 2, (rgt, lft, from_left, from_right), "middle", before)


def nothing(*refs):
    pass


def after(value, *others):
    return pl.pallas_call(
        nothing,
        out_shape=jax.ShapeDtypeStruct(value.shape, value.dtype),
        in_specs=[ANY] * (1 + len(others)),
        out_specs=ANY,
        input_output_aliases={0: 0},
        compiler_params=PARAMS,
        cost_estimate=pl.CostEstimate(flops=0, bytes_accessed=0, transcendentals=0),
        name="after",
    )(value, *others)


def total_kernel(z_ref, *refs):
    out_ref = refs[-1]
    for i, start in enumerate((z_ref[0] * 128, (1 - z_ref[0]) * 128)):
        own, *halves = refs[5 * i : 5 * i + 5]
        for half in range(2):
            value = own[pl.ds(half * 64, 64), :].astype(F32)
            for ref in halves[half::2]:
                value = value + ref[...].astype(F32)
            out_ref[pl.ds(pl.multiple_of(start + half * 64, 64), 64), :] = value.astype(BF)


def total(z, near, far):
    width = near[0].shape[1]
    return pl.pallas_call(
        total_kernel,
        out_shape=jax.ShapeDtypeStruct((256, width), BF),
        in_specs=[SMEM] + [VMEM] * 10,
        out_specs=VMEM,
        compiler_params=PARAMS,
        cost_estimate=pl.CostEstimate(flops=0, bytes_accessed=0, transcendentals=0),
        name="total",
    )(z, *near, *far)


def finish_kernel(back_ref, expert_ref, slot_ref, out_ref):
    returned = (back_ref[:128, :].astype(F32) + back_ref[128:, :].astype(F32)).astype(BF)
    out_ref[...] = dot(returned, placing_of(expert_ref[...], slot_ref[...]), 0, 0).astype(BF)


def finish(back, expert, slot):
    width = back.shape[1]
    outs = (((width, 128), BF),)
    return call(finish_kernel, outs, (back, expert, slot), "finish")[0]


def weights_kernel(*refs):
    pieces, factors = refs[:8], refs[8:12]
    out, rows, b, blocks, sems, b_sems, out_sems = refs[12:]
    width = out.shape[0]
    cut = 1024
    loads = []
    for part, at in enumerate((pl.ds(0, cut), pl.ds(cut, width - cut))):
        loads.append(
            [
                pltpu.make_async_copy(piece.at[:, at], rows.at[pl.ds(i * 128, 128), at], sems.at[part * 8 + i])
                for i, piece in enumerate(pieces)
            ]
        )
    loads[0] += [
        pltpu.make_async_copy(factor, b.at[pl.ds(start, factor.shape[0]), :], b_sems.at[i])
        for i, (factor, start) in enumerate(zip(factors, (0, 384, 512, 896)))
    ]
    for part in loads:
        for copy in part:
            copy.start()
    writes = []
    for i, start in enumerate(range(0, width, 256)):
        if start in (0, cut):
            for copy in loads[start // cut]:
                copy.wait()
        size = min(256, width - start)
        if i >= 2:
            writes[i - 2].wait()
        block = blocks.at[i % 2, pl.ds(0, size), :]
        block[...] = dot(rows[:, pl.ds(start, size)], b[...], 0, 0).astype(BF)
        writes.append(pltpu.make_async_copy(block, out.at[pl.ds(start, size), :], out_sems.at[i % 2]))
        writes[i].start()
    for write in writes[-2:]:
        write.wait()


def weights(pieces, factors):
    width, units = pieces[0].shape[1], factors[0].shape[1]
    args = [pltpu.with_memory_space_constraint(a, pltpu.HBM) for a in (*pieces, *factors)]
    return pl.pallas_call(
        weights_kernel,
        out_shape=pltpu.HBM((width, units), BF),
        in_specs=[pl.BlockSpec(memory_space=pltpu.HBM)] * 12,
        out_specs=pl.BlockSpec(memory_space=pltpu.HBM),
        scratch_shapes=[
            pltpu.VMEM((1024, width), BF),
            pltpu.VMEM((1024, units), BF),
            pltpu.VMEM((2, 256, units), BF),
            pltpu.SemaphoreType.DMA((16,)),
            pltpu.SemaphoreType.DMA((4,)),
            pltpu.SemaphoreType.DMA((2,)),
        ],
        compiler_params=PARAMS,
        cost_estimate=pl.CostEstimate(
            flops=2 * 1024 * width * units, bytes_accessed=10 << 20, transcendentals=0
        ),
        name="weights",
    )(*args)


def move(value, axis, pairs):
    blocks = value.reshape(-1, 64, value.shape[1])
    return lax.ppermute(blocks, axis, pairs).reshape(value.shape)


def right(value):
    return move(value, "x", RIGHT)


def left(value):
    return move(value, "x", LEFT)


def opposite(value):
    return move(value, "x", ACROSS)


def other_z(value):
    return move(value, "zl", SWAP)


def exchange(value, axes):
    blocks = value.reshape(-1, 8, value.shape[1])
    return lax.all_to_all(blocks, axes, split_axis=0, concat_axis=0, tiled=True).reshape(value.shape)


def per_device(grad_out, expert_id, slot, gate_prob, saved_inputs, w_in, w_out):
    width = grad_out.shape[1]
    expert = expert_id.reshape(1, -1)
    place = slot.reshape(1, -1)
    first = w_in[0]
    second = w_out[0].T
    z = lax.axis_index("zl").astype(jnp.int32).reshape(1)

    x_own = saved_inputs[0].reshape(128, width)
    x_lft, x_rgt, x_far, xz_own = right(x_own), left(x_own), opposite(x_own), other_z(x_own)
    g_own = exchange(prepare(grad_out.T, expert, place, gate_prob.reshape(1, -1)), WIDE)
    g_own = after(g_own, x_lft, x_rgt, x_far, xz_own)

    g_lft, g_rgt, gz_own = right(g_own), left(g_own), other_z(g_own)
    xz_lft = other_z(x_lft)

    gz_own = after(gz_own, g_lft, g_rgt)
    gz_lft, g_far, xz_far = right(gz_own), left(g_rgt), other_z(x_far)
    hidden_b, dhidden_b, partials = layer(
        (x_own, x_lft, x_rgt), (g_own, g_lft, g_rgt), first, second, (128, 64, 64, 64, 64)
    )

    gz_lft = after(gz_lft, g_far)
    gz_own = after(gz_own, gz_lft)
    gz_far, gz_rgt, xz_rgt = right(gz_lft), left(gz_own), other_z(x_rgt)
    p_own, lft0, lft1, rgt0, rgt1 = partials
    s_lft1, s_rgt0 = right(rgt1), left(lft0)
    hidden_a, dhidden_a, (far0, far1) = layer((x_far,), (g_far,), first, second, (64, 64), (s_lft1, s_rgt0))
    arrived = right(far0), left(far1)
    hidden_az, dhidden_az, (far0, far1) = layer((xz_far,), (gz_far,), first, second, (64, 64), (gz_rgt, xz_lft))
    rgt0, lft1 = middle(rgt0, lft1, *arrived, (hidden_az,))
    summands = p_own, right(rgt0), s_lft1, s_rgt0, left(lft1)
    hidden_bz, dhidden_bz, partials_z = layer(
        (xz_own, xz_lft, xz_rgt), (gz_own, gz_lft, gz_rgt), first, second, (128, 64, 64, 64, 64), (dhidden_az,)
    )
    pz_own, lft0, lft1, rgt0, rgt1 = partials_z
    s_lft1, s_rgt0 = right(rgt1), left(lft0)
    rgt0, lft1 = middle(rgt0, lft1, right(far0), left(far1), summands[1:])
    summands_z = pz_own, right(rgt0), s_lft1, s_rgt0, left(lft1)
    g_all = (g_own, g_lft, g_rgt, g_far, gz_own, gz_lft, gz_rgt, gz_far)
    x_all = (x_own, x_lft, x_rgt, x_far, xz_own, xz_lft, xz_rgt, xz_far)
    grad_out_w = weights(g_all, (hidden_b, hidden_a, hidden_bz, hidden_az))
    grad_in = weights(x_all, (dhidden_b, dhidden_a, dhidden_bz, dhidden_az))
    came_back = exchange(total(z, summands, summands_z), WIDE_AND_Z)
    tokens = finish(came_back, expert, place)
    return (tokens.T, grad_in[None], grad_out_w.T[None])


def solution(mesh):
    fine = Mesh(mesh.devices.reshape(4, 2, 2, 4, 2), AXES)
    every = WIDE + LOCAL
    placed = (
        P(every, None),
        P(every),
        P(every),
        P(every),
        P(WIDE, None, LOCAL, None),
        P(WIDE, None, LOCAL),
        P(WIDE, LOCAL, None),
    )
    return jax.shard_map(
        per_device,
        mesh=fine,
        in_specs=placed,
        out_specs=(P(every, None), P(WIDE, None, LOCAL), P(WIDE, LOCAL, None)),
        check_vma=False,
    )
```

```python
import functools

import jax
import jax.numpy as jnp
from jax import lax
from jax.experimental import pallas as pl
from jax.experimental.pallas import tpu as pltpu
from jax.sharding import Mesh, PartitionSpec as P

AXES = ("y", "zh", "core", "x", "zl")
WIDE = ("y", "zh", "core")
LOCAL = ("x", "zl")
WIDE_AND_Z = ("zl",) + WIDE
RIGHT = [(i, (i + 1) % 4) for i in range(4)]
LEFT = [(i, (i - 1) % 4) for i in range(4)]
ACROSS = [(i, (i + 2) % 4) for i in range(4)]
SWAP = [(0, 1), (1, 0)]
BF = jnp.bfloat16
F32 = jnp.float32
VMEM = pl.BlockSpec(memory_space=pltpu.VMEM)
ANY = pl.BlockSpec(memory_space=pl.ANY)
SMEM = pl.BlockSpec(memory_space=pltpu.SMEM)
PARAMS = pltpu.CompilerParams(vmem_limit_bytes=14 * 1024 * 1024)


def dot(a, b, da, db):
    return lax.dot_general(a, b, (((da,), (db,)), ((), ())), preferred_element_type=F32)


def call(kernel, outs, args, name, after=()):
    def ordered(*refs):
        kernel(*refs[: len(args)], *refs[len(args) + len(after) :])

    return pl.pallas_call(
        ordered,
        out_shape=tuple(jax.ShapeDtypeStruct(s, d) for s, d in outs),
        in_specs=[VMEM] * len(args) + [ANY] * len(after),
        out_specs=(VMEM,) * len(outs),
        compiler_params=PARAMS,
        cost_estimate=pl.CostEstimate(flops=0, bytes_accessed=4 << 20, transcendentals=0),
        name=name,
    )(*args, *after)


def stacked(refs):
    return jnp.concatenate([ref[...] for ref in refs], axis=0)


def placing_of(expert, slot):
    target = jnp.where(slot >= 0, expert * 8 + slot, -1)
    rows = lax.broadcasted_iota(jnp.int32, (128, 128), 0)
    return jnp.where(rows == target, 1.0, 0.0).astype(BF)


def prepare_kernel(grad, expert, slot, gate, out_ref, grad_ref, expert_ref, slot_ref, gate_ref, sems):
    pairs = ((grad, grad_ref), (expert, expert_ref), (slot, slot_ref), (gate, gate_ref))
    copies = [pltpu.make_async_copy(src, dst, sems.at[i]) for i, (src, dst) in enumerate(pairs)]
    for copy in copies:
        copy.start()
    for copy in copies:
        copy.wait()
    scaled = (gate_ref[...] * grad_ref[...].astype(F32)).astype(BF)
    outgoing = dot(placing_of(expert_ref[...], slot_ref[...]), scaled, 1, 1).astype(BF)
    out_ref[...] = outgoing


def prepare(*args):
    width = args[0].shape[0]
    args = [pltpu.with_memory_space_constraint(a, pltpu.HBM) for a in args]
    return pl.pallas_call(
        prepare_kernel,
        out_shape=jax.ShapeDtypeStruct((128, width), BF),
        in_specs=[pl.BlockSpec(memory_space=pltpu.HBM)] * 4,
        out_specs=VMEM,
        scratch_shapes=[pltpu.VMEM(a.shape, a.dtype) for a in args] + [pltpu.SemaphoreType.DMA((4,))],
        compiler_params=PARAMS,
        cost_estimate=pl.CostEstimate(
            flops=2 * 128 * 128 * width, bytes_accessed=8 * 128 * width, transcendentals=0
        ),
        name="prepare",
    )(*args)


def gelu_parts(value):
    normal_cdf = 0.5 * (1.0 + lax.erf(value * 0.7071067811865476))
    density = jnp.exp(-0.5 * value * value) * 0.3989422804014327
    return value * normal_cdf, normal_cdf + value * density


def layer_kernel(count, *refs):
    x, g = refs[:count], refs[count : 2 * count]
    wi_ref, wo_ref, hidden_ref, dhidden_ref, *outs = refs[2 * count :]
    value, slope = gelu_parts(dot(stacked(x), wi_ref[...], 1, 0))
    hidden_ref[...] = value.astype(BF)
    dhidden = (dot(stacked(g), wo_ref[...], 1, 0) * slope).astype(BF)
    dhidden_ref[...] = dhidden
    partial_value = dot(dhidden, wi_ref[...], 1, 1).astype(BF)
    start = 0
    for out in outs:
        size = out.shape[0]
        out[...] = partial_value[start : start + size]
        start += size


def layer(x, g, w_in, w_out_t, sizes, before=()):
    width, units = w_in.shape
    rows = 128 * len(x)
    outs = (((rows, units), BF),) * 2 + tuple(((size, width), BF) for size in sizes)
    kernel = functools.partial(layer_kernel, len(x))
    hidden, dhidden, *partials = call(kernel, outs, (*x, *g, w_in, w_out_t), "layer", before)
    return hidden, dhidden, partials


def forward_kernel(own, lft, far, wi_ref, hidden_ref, hidden_far_ref, slope_ref, slope_far_ref):
    value, slope = gelu_parts(dot(stacked((own, lft, far)), wi_ref[...], 1, 0))
    hidden_ref[...] = value[:256].astype(BF)
    hidden_far_ref[...] = value[256:].astype(BF)
    slope_ref[...] = slope[:256]
    slope_far_ref[...] = slope[256:]


def forward(own, lft, far, w_in):
    units = w_in.shape[1]
    outs = tuple(((rows, units), dtype) for dtype in (BF, F32) for rows in (256, 128))
    return call(forward_kernel, outs, (own, lft, far, w_in), "forward")


def far_kernel(g, slope_ref, wi_ref, wo_ref, dhidden_ref, out0, out1):
    dhidden = (dot(g[...], wo_ref[...], 1, 0) * slope_ref[...]).astype(BF)
    dhidden_ref[...] = dhidden
    partial_value = dot(dhidden, wi_ref[...], 1, 1).astype(BF)
    out0[...] = partial_value[:64]
    out1[...] = partial_value[64:]


def far_layer(g, slope, w_in, w_out_t, before):
    width, units = w_in.shape
    outs = (((128, units), BF),) + (((64, width), BF),) * 2
    return call(far_kernel, outs, (g, slope, w_in, w_out_t), "far_layer", before)


def rest_kernel(x, own, lft, rgt, slope_ref, wi_ref, wo_ref, hidden_ref, dhidden_ref, *outs):
    value, slope = gelu_parts(dot(x[...], wi_ref[...], 1, 0))
    hidden_ref[...] = value.astype(BF)
    slope = jnp.concatenate([slope_ref[...], slope], axis=0)
    dhidden = (dot(stacked((own, lft, rgt)), wo_ref[...], 1, 0) * slope).astype(BF)
    dhidden_ref[...] = dhidden
    partial_value = dot(dhidden, wi_ref[...], 1, 1).astype(BF)
    outs[0][...] = partial_value[:128]
    for i, out in enumerate(outs[1:]):
        out[...] = partial_value[128 + 64 * i : 192 + 64 * i]


def rest_layer(x, g, slope, w_in, w_out_t, before):
    width, units = w_in.shape
    outs = (((128, units), BF), ((384, units), BF), ((128, width), BF)) + (((64, width), BF),) * 4
    return call(rest_kernel, outs, (x, *g, slope, w_in, w_out_t), "rest_layer", before)


def middle_kernel(rgt, lft, far0, far1, rgt_out, lft_out):
    rgt_out[...] = (rgt[...].astype(F32) + far0[...].astype(F32)).astype(BF)
    lft_out[...] = (lft[...].astype(F32) + far1[...].astype(F32)).astype(BF)


def middle(rgt, lft, from_left, from_right, before=()):
    return call(middle_kernel, ((rgt.shape, BF),) * 2, (rgt, lft, from_left, from_right), "middle", before)


def nothing(*refs):
    pass


def after(value, *others):
    return pl.pallas_call(
        nothing,
        out_shape=jax.ShapeDtypeStruct(value.shape, value.dtype),
        in_specs=[ANY] * (1 + len(others)),
        out_specs=ANY,
        input_output_aliases={0: 0},
        compiler_params=PARAMS,
        cost_estimate=pl.CostEstimate(flops=0, bytes_accessed=0, transcendentals=0),
        name="after",
    )(value, *others)


def total_kernel(z_ref, *refs):
    out_ref = refs[-1]
    for i, start in enumerate((z_ref[0] * 128, (1 - z_ref[0]) * 128)):
        own, *halves = refs[5 * i : 5 * i + 5]
        for half in range(2):
            value = own[pl.ds(half * 64, 64), :].astype(F32)
            for ref in halves[half::2]:
                value = value + ref[...].astype(F32)
            out_ref[pl.ds(pl.multiple_of(start + half * 64, 64), 64), :] = value.astype(BF)


def total(z, near, far):
    width = near[0].shape[1]
    return pl.pallas_call(
        total_kernel,
        out_shape=jax.ShapeDtypeStruct((256, width), BF),
        in_specs=[SMEM] + [VMEM] * 10,
        out_specs=VMEM,
        compiler_params=PARAMS,
        cost_estimate=pl.CostEstimate(flops=0, bytes_accessed=0, transcendentals=0),
        name="total",
    )(z, *near, *far)


def finish_kernel(back_ref, expert_ref, slot_ref, out_ref):
    returned = (back_ref[:128, :].astype(F32) + back_ref[128:, :].astype(F32)).astype(BF)
    out_ref[...] = dot(returned, placing_of(expert_ref[...], slot_ref[...]), 0, 0).astype(BF)


def finish(back, expert, slot):
    width = back.shape[1]
    outs = (((width, 128), BF),)
    return call(finish_kernel, outs, (back, expert, slot), "finish")[0]


def weights_kernel(*refs):
    pieces, factors = refs[:8], refs[8:-7]
    out, rows, b, blocks, sems, b_sems, out_sems = refs[-7:]
    width = out.shape[0]
    cut = 1024
    loads = []
    for part, at in enumerate((pl.ds(0, cut), pl.ds(cut, width - cut))):
        loads.append(
            [
                pltpu.make_async_copy(piece.at[:, at], rows.at[pl.ds(i * 128, 128), at], sems.at[part * 8 + i])
                for i, piece in enumerate(pieces)
            ]
        )
    start = 0
    for i, factor in enumerate(factors):
        size = factor.shape[0]
        loads[0].append(pltpu.make_async_copy(factor, b.at[pl.ds(start, size), :], b_sems.at[i]))
        start += size
    for part in loads:
        for copy in part:
            copy.start()
    writes = []
    for i, start in enumerate(range(0, width, 256)):
        if start in (0, cut):
            for copy in loads[start // cut]:
                copy.wait()
        size = min(256, width - start)
        if i >= 2:
            writes[i - 2].wait()
        block = blocks.at[i % 2, pl.ds(0, size), :]
        block[...] = dot(rows[:, pl.ds(start, size)], b[...], 0, 0).astype(BF)
        writes.append(pltpu.make_async_copy(block, out.at[pl.ds(start, size), :], out_sems.at[i % 2]))
        writes[i].start()
    for write in writes[-2:]:
        write.wait()


def weights(pieces, factors):
    width, units = pieces[0].shape[1], factors[0].shape[1]
    args = [pltpu.with_memory_space_constraint(a, pltpu.HBM) for a in (*pieces, *factors)]
    return pl.pallas_call(
        weights_kernel,
        out_shape=pltpu.HBM((width, units), BF),
        in_specs=[pl.BlockSpec(memory_space=pltpu.HBM)] * len(args),
        out_specs=pl.BlockSpec(memory_space=pltpu.HBM),
        scratch_shapes=[
            pltpu.VMEM((1024, width), BF),
            pltpu.VMEM((1024, units), BF),
            pltpu.VMEM((2, 256, units), BF),
            pltpu.SemaphoreType.DMA((16,)),
            pltpu.SemaphoreType.DMA((len(factors),)),
            pltpu.SemaphoreType.DMA((2,)),
        ],
        compiler_params=PARAMS,
        cost_estimate=pl.CostEstimate(
            flops=2 * 1024 * width * units, bytes_accessed=10 << 20, transcendentals=0
        ),
        name="weights",
    )(*args)


def move(value, axis, pairs):
    blocks = value.reshape(-1, 64, value.shape[1])
    return lax.ppermute(blocks, axis, pairs).reshape(value.shape)


def right(value):
    return move(value, "x", RIGHT)


def left(value):
    return move(value, "x", LEFT)


def opposite(value):
    return move(value, "x", ACROSS)


def other_z(value):
    return move(value, "zl", SWAP)


def exchange(value, axes):
    blocks = value.reshape(-1, 8, value.shape[1])
    return lax.all_to_all(blocks, axes, split_axis=0, concat_axis=0, tiled=True).reshape(value.shape)


def per_device(grad_out, expert_id, slot, gate_prob, saved_inputs, w_in, w_out):
    width = grad_out.shape[1]
    expert = expert_id.reshape(1, -1)
    place = slot.reshape(1, -1)
    first = w_in[0]
    second = w_out[0].T
    z = lax.axis_index("zl").astype(jnp.int32).reshape(1)

    x_own = saved_inputs[0].reshape(128, width)
    x_lft, x_rgt, x_far, xz_own = right(x_own), left(x_own), opposite(x_own), other_z(x_own)
    g_own = exchange(prepare(grad_out.T, expert, place, gate_prob.reshape(1, -1)), WIDE)
    g_own = after(g_own, x_lft, x_rgt, x_far, xz_own)

    g_lft, g_rgt, gz_own = right(g_own), left(g_own), other_z(g_own)
    xz_lft = other_z(x_lft)

    gz_own = after(gz_own, g_lft)
    gz_lft, g_far, xz_far = right(gz_own), left(g_rgt), other_z(x_far)
    hidden_b, dhidden_b, partials = layer(
        (x_own, x_lft, x_rgt), (g_own, g_lft, g_rgt), first, second, (128, 64, 64, 64, 64)
    )

    gz_lft = after(gz_lft, g_far)
    gz_own = after(gz_own, gz_lft)
    gz_far, gz_rgt, xz_rgt = right(gz_lft), left(gz_own), other_z(x_rgt)
    p_own, lft0, lft1, rgt0, rgt1 = partials
    s_lft1, s_rgt0 = right(rgt1), left(lft0)
    hidden_a, dhidden_a, (far0, far1) = layer((x_far,), (g_far,), first, second, (64, 64), (s_lft1, s_rgt0, ))
    arrived = right(far0), left(far1)
    hidden_bz, hidden_az, slope, slope_far = forward(xz_own, xz_lft, xz_far, first)
    dhidden_az, far0, far1 = far_layer(gz_far, slope_far, first, second, (gz_rgt,))
    rgt0, lft1 = middle(rgt0, lft1, *arrived, (dhidden_az,))
    summands = p_own, right(rgt0), s_lft1, s_rgt0, left(lft1)
    hidden_cz, dhidden_bz, pz_own, lft0, lft1, rgt0, rgt1 = rest_layer(
        xz_rgt, (gz_own, gz_lft, gz_rgt), slope, first, second, (dhidden_az,)
    )
    sz_lft1, sz_rgt0 = right(rgt1), left(lft0)
    rgt0, lft1 = middle(rgt0, lft1, right(far0), left(far1), (*summands[1:], ))
    summands_z = pz_own, right(rgt0), sz_lft1, sz_rgt0, left(lft1)
    g_all = (g_own, g_lft, g_rgt, g_far, gz_own, gz_lft, gz_rgt, gz_far)
    x_all = (x_own, x_lft, x_rgt, x_far, xz_own, xz_lft, xz_rgt, xz_far)
    grad_out_w = weights(g_all, (hidden_b, hidden_a, hidden_bz, hidden_cz, hidden_az))
    grad_in = weights(x_all, (dhidden_b, dhidden_a, dhidden_bz, dhidden_az))
    came_back = exchange(total(z, summands, summands_z), WIDE_AND_Z)
    tokens = finish(came_back, expert, place)
    return (tokens.T, grad_in[None], grad_out_w.T[None])


def solution(mesh):
    fine = Mesh(mesh.devices.reshape(4, 2, 2, 4, 2), AXES)
    every = WIDE + LOCAL
    placed = (
        P(every, None),
        P(every),
        P(every),
        P(every),
        P(WIDE, None, LOCAL, None),
        P(WIDE, None, LOCAL),
        P(WIDE, LOCAL, None),
    )
    return jax.shard_map(
        per_device,
        mesh=fine,
        in_specs=placed,
        out_specs=(P(every, None), P(WIDE, None, LOCAL), P(WIDE, LOCAL, None)),
        check_vma=False,
    )
```

```python
import functools

import jax
import jax.numpy as jnp
from jax import lax
from jax.experimental import pallas as pl
from jax.experimental.pallas import tpu as pltpu
from jax.sharding import Mesh, PartitionSpec as P

AXES = ("y", "zh", "core", "x", "zl")
WIDE = ("y", "zh", "core")
LOCAL = ("x", "zl")
WIDE_AND_Z = ("zl",) + WIDE
RIGHT = [(i, (i + 1) % 4) for i in range(4)]
LEFT = [(i, (i - 1) % 4) for i in range(4)]
ACROSS = [(i, (i + 2) % 4) for i in range(4)]
SWAP = [(0, 1), (1, 0)]
BF = jnp.bfloat16
F32 = jnp.float32
VMEM = pl.BlockSpec(memory_space=pltpu.VMEM)
ANY = pl.BlockSpec(memory_space=pl.ANY)
SMEM = pl.BlockSpec(memory_space=pltpu.SMEM)
PARAMS = pltpu.CompilerParams(vmem_limit_bytes=14 * 1024 * 1024)


def dot(a, b, da, db):
    return lax.dot_general(a, b, (((da,), (db,)), ((), ())), preferred_element_type=F32)


def call(kernel, outs, args, name, after=()):
    def ordered(*refs):
        kernel(*refs[: len(args)], *refs[len(args) + len(after) :])

    return pl.pallas_call(
        ordered,
        out_shape=tuple(jax.ShapeDtypeStruct(s, d) for s, d in outs),
        in_specs=[VMEM] * len(args) + [ANY] * len(after),
        out_specs=(VMEM,) * len(outs),
        compiler_params=PARAMS,
        cost_estimate=pl.CostEstimate(flops=0, bytes_accessed=4 << 20, transcendentals=0),
        name=name,
    )(*args, *after)


def stacked(refs):
    return jnp.concatenate([ref[...] for ref in refs], axis=0)


def placing_of(expert, slot):
    target = jnp.where(slot >= 0, expert * 8 + slot, -1)
    rows = lax.broadcasted_iota(jnp.int32, (128, 128), 0)
    return jnp.where(rows == target, 1.0, 0.0).astype(BF)


def prepare_kernel(grad, expert, slot, gate, out_ref, grad_ref, expert_ref, slot_ref, gate_ref, sems):
    pairs = ((grad, grad_ref), (expert, expert_ref), (slot, slot_ref), (gate, gate_ref))
    copies = [pltpu.make_async_copy(src, dst, sems.at[i]) for i, (src, dst) in enumerate(pairs)]
    for copy in copies:
        copy.start()
    for copy in copies:
        copy.wait()
    scaled = (gate_ref[...] * grad_ref[...].astype(F32)).astype(BF)
    outgoing = dot(placing_of(expert_ref[...], slot_ref[...]), scaled, 1, 1).astype(BF)
    out_ref[...] = outgoing


def prepare(*args):
    width = args[0].shape[0]
    args = [pltpu.with_memory_space_constraint(a, pltpu.HBM) for a in args]
    return pl.pallas_call(
        prepare_kernel,
        out_shape=jax.ShapeDtypeStruct((128, width), BF),
        in_specs=[pl.BlockSpec(memory_space=pltpu.HBM)] * 4,
        out_specs=VMEM,
        scratch_shapes=[pltpu.VMEM(a.shape, a.dtype) for a in args] + [pltpu.SemaphoreType.DMA((4,))],
        compiler_params=PARAMS,
        cost_estimate=pl.CostEstimate(
            flops=2 * 128 * 128 * width, bytes_accessed=8 * 128 * width, transcendentals=0
        ),
        name="prepare",
    )(*args)


def gelu_parts(value):
    normal_cdf = 0.5 * (1.0 + lax.erf(value * 0.7071067811865476))
    density = jnp.exp(-0.5 * value * value) * 0.3989422804014327
    return value * normal_cdf, normal_cdf + value * density


def layer_kernel(count, *refs):
    x, g = refs[:count], refs[count : 2 * count]
    wi_ref, wo_ref, hidden_ref, dhidden_ref, *outs = refs[2 * count :]
    value, slope = gelu_parts(dot(stacked(x), wi_ref[...], 1, 0))
    hidden_ref[...] = value.astype(BF)
    dhidden = (dot(stacked(g), wo_ref[...], 1, 0) * slope).astype(BF)
    dhidden_ref[...] = dhidden
    partial_value = dot(dhidden, wi_ref[...], 1, 1).astype(BF)
    start = 0
    for out in outs:
        size = out.shape[0]
        out[...] = partial_value[start : start + size]
        start += size


def layer(x, g, w_in, w_out_t, sizes, before=()):
    width, units = w_in.shape
    rows = 128 * len(x)
    outs = (((rows, units), BF),) * 2 + tuple(((size, width), BF) for size in sizes)
    kernel = functools.partial(layer_kernel, len(x))
    hidden, dhidden, *partials = call(kernel, outs, (*x, *g, w_in, w_out_t), "layer", before)
    return hidden, dhidden, partials


def forward_kernel(own, lft, far, wi_ref, hidden_ref, hidden_far_ref, slope_ref, slope_far_ref):
    value, slope = gelu_parts(dot(stacked((own, lft, far)), wi_ref[...], 1, 0))
    hidden_ref[...] = value[:256].astype(BF)
    hidden_far_ref[...] = value[256:].astype(BF)
    slope_ref[...] = slope[:256]
    slope_far_ref[...] = slope[256:]


def forward(own, lft, far, w_in):
    units = w_in.shape[1]
    outs = tuple(((rows, units), dtype) for dtype in (BF, F32) for rows in (256, 128))
    return call(forward_kernel, outs, (own, lft, far, w_in), "forward")


def far_kernel(g, slope_ref, wi_ref, wo_ref, dhidden_ref, out0, out1):
    dhidden = (dot(g[...], wo_ref[...], 1, 0) * slope_ref[...]).astype(BF)
    dhidden_ref[...] = dhidden
    partial_value = dot(dhidden, wi_ref[...], 1, 1).astype(BF)
    out0[...] = partial_value[:64]
    out1[...] = partial_value[64:]


def far_layer(g, slope, w_in, w_out_t, before):
    width, units = w_in.shape
    outs = (((128, units), BF),) + (((64, width), BF),) * 2
    return call(far_kernel, outs, (g, slope, w_in, w_out_t), "far_layer", before)


def rest_kernel(x, own, lft, rgt, slope_ref, wi_ref, wo_ref, hidden_ref, dhidden_ref, *outs):
    value, slope = gelu_parts(dot(x[...], wi_ref[...], 1, 0))
    hidden_ref[...] = value.astype(BF)
    slope = jnp.concatenate([slope_ref[...], slope], axis=0)
    dhidden = (dot(stacked((own, lft, rgt)), wo_ref[...], 1, 0) * slope).astype(BF)
    dhidden_ref[...] = dhidden
    partial_value = dot(dhidden, wi_ref[...], 1, 1).astype(BF)
    outs[0][...] = partial_value[:128]
    for i, out in enumerate(outs[1:]):
        out[...] = partial_value[128 + 64 * i : 192 + 64 * i]


def rest_layer(x, g, slope, w_in, w_out_t, before):
    width, units = w_in.shape
    outs = (((128, units), BF), ((384, units), BF), ((128, width), BF)) + (((64, width), BF),) * 4
    return call(rest_kernel, outs, (x, *g, slope, w_in, w_out_t), "rest_layer", before)


def middle_kernel(rgt, lft, far0, far1, rgt_out, lft_out):
    rgt_out[...] = (rgt[...].astype(F32) + far0[...].astype(F32)).astype(BF)
    lft_out[...] = (lft[...].astype(F32) + far1[...].astype(F32)).astype(BF)


def middle(rgt, lft, from_left, from_right, before=()):
    return call(middle_kernel, ((rgt.shape, BF),) * 2, (rgt, lft, from_left, from_right), "middle", before)


def nothing(*refs):
    pass


def after(value, *others):
    return pl.pallas_call(
        nothing,
        out_shape=jax.ShapeDtypeStruct(value.shape, value.dtype),
        in_specs=[ANY] * (1 + len(others)),
        out_specs=ANY,
        input_output_aliases={0: 0},
        compiler_params=PARAMS,
        cost_estimate=pl.CostEstimate(flops=0, bytes_accessed=0, transcendentals=0),
        name="after",
    )(value, *others)


def sum_kernel(own, lft0, lft1, rgt0, rgt1, out_ref):
    for half, (lft, rgt) in enumerate(((lft0, rgt0), (lft1, rgt1))):
        at = pl.ds(half * 64, 64)
        value = own[at, :].astype(F32) + lft[...].astype(F32) + rgt[...].astype(F32)
        out_ref[at, :] = value.astype(BF)


def total_kernel(z_ref, near, own, lft0, lft1, rgt0, rgt1, out_ref):
    out_ref[pl.ds(pl.multiple_of(z_ref[0] * 128, 128), 128), :] = near[...]
    for half, (lft, rgt) in enumerate(((lft0, rgt0), (lft1, rgt1))):
        value = own[pl.ds(half * 64, 64), :].astype(F32) + lft[...].astype(F32) + rgt[...].astype(F32)
        start = pl.multiple_of((1 - z_ref[0]) * 128 + half * 64, 64)
        out_ref[pl.ds(start, 64), :] = value.astype(BF)


def total(z, near, far):
    width = near[0].shape[1]
    near = call(sum_kernel, (((128, width), BF),), near, "near_sum")[0]
    return pl.pallas_call(
        total_kernel,
        out_shape=jax.ShapeDtypeStruct((256, width), BF),
        in_specs=[SMEM] + [VMEM] * 6,
        out_specs=VMEM,
        compiler_params=PARAMS,
        cost_estimate=pl.CostEstimate(flops=0, bytes_accessed=0, transcendentals=0),
        name="total",
    )(z, near, *far)


def finish_kernel(back_ref, expert_ref, slot_ref, out_ref):
    returned = (back_ref[:128, :].astype(F32) + back_ref[128:, :].astype(F32)).astype(BF)
    out_ref[...] = dot(returned, placing_of(expert_ref[...], slot_ref[...]), 0, 0).astype(BF)


def finish(back, expert, slot):
    width = back.shape[1]
    outs = (((width, 128), BF),)
    return call(finish_kernel, outs, (back, expert, slot), "finish")[0]


def weights_kernel(*refs):
    pieces, factors = refs[:8], refs[8:-7]
    out, rows, b, blocks, sems, b_sems, out_sems = refs[-7:]
    width = out.shape[0]
    cut = 1024
    loads = []
    for part, at in enumerate((pl.ds(0, cut), pl.ds(cut, width - cut))):
        loads.append(
            [
                pltpu.make_async_copy(piece.at[:, at], rows.at[pl.ds(i * 128, 128), at], sems.at[part * 8 + i])
                for i, piece in enumerate(pieces)
            ]
        )
    start = 0
    for i, factor in enumerate(factors):
        size = factor.shape[0]
        loads[0].append(pltpu.make_async_copy(factor, b.at[pl.ds(start, size), :], b_sems.at[i]))
        start += size
    for part in loads:
        for copy in part:
            copy.start()
    writes = []
    for i, start in enumerate(range(0, width, 256)):
        if start in (0, cut):
            for copy in loads[start // cut]:
                copy.wait()
        size = min(256, width - start)
        if i >= 2:
            writes[i - 2].wait()
        block = blocks.at[i % 2, pl.ds(0, size), :]
        block[...] = dot(rows[:, pl.ds(start, size)], b[...], 0, 0).astype(BF)
        writes.append(pltpu.make_async_copy(block, out.at[pl.ds(start, size), :], out_sems.at[i % 2]))
        writes[i].start()
    for write in writes[-2:]:
        write.wait()


def weights(pieces, factors):
    width, units = pieces[0].shape[1], factors[0].shape[1]
    args = [pltpu.with_memory_space_constraint(a, pltpu.HBM) for a in (*pieces, *factors)]
    return pl.pallas_call(
        weights_kernel,
        out_shape=pltpu.HBM((width, units), BF),
        in_specs=[pl.BlockSpec(memory_space=pltpu.HBM)] * len(args),
        out_specs=pl.BlockSpec(memory_space=pltpu.HBM),
        scratch_shapes=[
            pltpu.VMEM((1024, width), BF),
            pltpu.VMEM((1024, units), BF),
            pltpu.VMEM((2, 256, units), BF),
            pltpu.SemaphoreType.DMA((16,)),
            pltpu.SemaphoreType.DMA((len(factors),)),
            pltpu.SemaphoreType.DMA((2,)),
        ],
        compiler_params=PARAMS,
        cost_estimate=pl.CostEstimate(
            flops=2 * 1024 * width * units, bytes_accessed=10 << 20, transcendentals=0
        ),
        name="weights",
    )(*args)


def move(value, axis, pairs):
    blocks = value.reshape(-1, 64, value.shape[1])
    return lax.ppermute(blocks, axis, pairs).reshape(value.shape)


def right(value):
    return move(value, "x", RIGHT)


def left(value):
    return move(value, "x", LEFT)


def opposite(value):
    return move(value, "x", ACROSS)


def other_z(value):
    return move(value, "zl", SWAP)


def exchange(value, axes):
    blocks = value.reshape(-1, 8, value.shape[1])
    return lax.all_to_all(blocks, axes, split_axis=0, concat_axis=0, tiled=True).reshape(value.shape)


def per_device(grad_out, expert_id, slot, gate_prob, saved_inputs, w_in, w_out):
    width = grad_out.shape[1]
    expert = expert_id.reshape(1, -1)
    place = slot.reshape(1, -1)
    first = w_in[0]
    second = w_out[0].T
    z = lax.axis_index("zl").astype(jnp.int32).reshape(1)

    x_own = saved_inputs[0].reshape(128, width)
    x_lft, x_rgt, x_far, xz_own = right(x_own), left(x_own), opposite(x_own), other_z(x_own)
    g_own = exchange(prepare(grad_out.T, expert, place, gate_prob.reshape(1, -1)), WIDE)
    g_own = after(g_own, x_lft, x_rgt, x_far, xz_own)

    g_lft, g_rgt, gz_own = right(g_own), left(g_own), other_z(g_own)
    xz_lft = other_z(x_lft)

    gz_own = after(gz_own, g_lft)
    gz_lft, g_far, xz_far = right(gz_own), left(g_rgt), other_z(x_far)
    hidden_b, dhidden_b, partials = layer(
        (x_own, x_lft, x_rgt), (g_own, g_lft, g_rgt), first, second, (128, 64, 64, 64, 64)
    )

    gz_lft = after(gz_lft, g_far)
    gz_own = after(gz_own, gz_lft)
    gz_far, gz_rgt, xz_rgt = right(gz_lft), left(gz_own), other_z(x_rgt)
    p_own, lft0, lft1, rgt0, rgt1 = partials
    s_lft1, s_rgt0 = right(rgt1), left(lft0)
    hidden_a, dhidden_a, (far0, far1) = layer((x_far,), (g_far,), first, second, (64, 64), (s_lft1, s_rgt0, ))
    arrived = right(far0), left(far1)
    hidden_bz, hidden_az, slope, slope_far = forward(xz_own, xz_lft, xz_far, first)
    dhidden_az, far0, far1 = far_layer(gz_far, slope_far, first, second, (gz_rgt,))
    rgt0, lft1 = middle(rgt0, lft1, *arrived, (dhidden_az,))
    summands = p_own, right(rgt0), s_lft1, s_rgt0, left(lft1)
    hidden_cz, dhidden_bz, pz_own, lft0, lft1, rgt0, rgt1 = rest_layer(
        xz_rgt, (gz_own, gz_lft, gz_rgt), slope, first, second, (dhidden_az,)
    )
    sz_lft1, sz_rgt0 = right(rgt1), left(lft0)
    rgt0, lft1 = middle(rgt0, lft1, right(far0), left(far1), (*summands[1:], ))
    summands_z = pz_own, right(rgt0), sz_lft1, sz_rgt0, left(lft1)
    g_all = (g_own, g_lft, g_rgt, g_far, gz_own, gz_lft, gz_rgt, gz_far)
    x_all = (x_own, x_lft, x_rgt, x_far, xz_own, xz_lft, xz_rgt, xz_far)
    grad_out_w = weights(g_all, (hidden_b, hidden_a, hidden_bz, hidden_cz, hidden_az))
    grad_in = weights(x_all, (dhidden_b, dhidden_a, dhidden_bz, dhidden_az))
    came_back = exchange(total(z, summands, summands_z), WIDE_AND_Z)
    tokens = finish(came_back, expert, place)
    return (tokens.T, grad_in[None], grad_out_w.T[None])


def solution(mesh):
    fine = Mesh(mesh.devices.reshape(4, 2, 2, 4, 2), AXES)
    every = WIDE + LOCAL
    placed = (
        P(every, None),
        P(every),
        P(every),
        P(every),
        P(WIDE, None, LOCAL, None),
        P(WIDE, None, LOCAL),
        P(WIDE, LOCAL, None),
    )
    return jax.shard_map(
        per_device,
        mesh=fine,
        in_specs=placed,
        out_specs=(P(every, None), P(WIDE, None, LOCAL), P(WIDE, LOCAL, None)),
        check_vma=False,
    )
```
